128 devices in a mesh: pipe: 8 (over z, core), expert: 16 (over y, x).
Axes of the slice: x: 4, y: 4, z: 4, core: 2. Of those that a mesh axis runs over, the one named last changes fastest.
Arguments:
- a_init: bfloat16 [8, 2048, 3584], P('pipe', 'expert'), may hold values from -6 to 6
- b_init: bfloat16 [8, 2048, 3584], P('pipe', 'expert'), may hold values from -6 to 6
- incoming: bfloat16 [1, 2048, 3584], P(None, 'expert'), may hold values from -6 to 6
- routes: int32 [8, 2, 2, 2048, 1], P('pipe', None, None, 'expert'), may hold values from 0 to 7; in each aligned block of 128 rows (0 to 127, 128 to 255, ..., all dimensions but the last counted through in order) at most 20 rows name the same one
- gain: bfloat16 [8, 2, 3584], P('pipe'), may hold values from 0.5 to 1.5
- router: bfloat16 [8, 2, 3584, 8], P('pipe'), may hold values from -0.09375 to 0.09375
- w_gate: bfloat16 [8, 2, 3584, 8192], P('pipe', None, None, 'expert'), may hold values from -0.09375 to 0.09375
- w_up: bfloat16 [8, 2, 3584, 8192], P('pipe', None, None, 'expert'), may hold values from -0.09375 to 0.09375
- w_down: bfloat16 [8, 2, 8192, 3584], P('pipe', None, 'expert'), may hold values from -0.1875 to 0.1875
Outputs:
- out_a: bfloat16 [2, 8, 2048, 3584], P(None, 'pipe', 'expert')
- out_b: bfloat16 [2, 8, 2048, 3584], P(None, 'pipe', 'expert')
The draws below stay inside these ranges and needn't reach their ends.
Inputs may be any that keep to these rules, and one draw needn't show every extreme that they name: `routes`: in each aligned block of 128 rows (one device's tokens of one slot and step) no expert is named more than 20 times, a bound that some block reaches.
All inputs are finite; a program needn't handle non-finite values.
Results may differ from the reference program's by a relative error of at most 0.014.
Values may be sent and summed in bfloat16 or wider, within the bound.
A program may use at most 192 MiB of HBM per device.

```python
import math
import jax
import jax.numpy as jnp
import numpy as np
from jax import lax

D = 3584
FF = 1024
SPLIT = 2
TOP = 1
STEPS = 2
TOK_DEV = 128
NEXP = 8
FF_DEV = 512
CAP = 20
TOKENS = 2048
N_PIPE = 8
N_EXPERT = 16


def levels(rng, dims, cuts, smallest, high):
    level, own = 1.0, jax.random.fold_in(rng, 6)
    for axis_at, parts in cuts:
        steps = jnp.exp(jax.random.uniform(jax.random.fold_in(own, axis_at), (parts,), jnp.float32, smallest / len(cuts), high / len(cuts)))
        level = level * jnp.repeat(steps, dims[axis_at] // parts).reshape([-1 if axis == axis_at else 1 for axis in range(len(dims))])
    return level


def routed_block(key, own, number, rows, count, top, bound, slope):
    ranking = jax.random.permutation(key, count)
    heavy_load, ordinary = shares(count, rows * top, bound, slope, True), shares(count, rows * top, bound, slope, False)
    places = jnp.arange(count)

    def named(tallies, rotation):
        used = int((tallies > 0).sum())
        fixed = max(1, used // 4)
        passed = fixed + (places - fixed + rotation * (used - fixed)) % max(1, count - fixed)
        return jnp.zeros((count,), jnp.int32).at[ranking[jnp.where(places < fixed, places, passed)]].set(jnp.asarray(tallies, jnp.int32))

    tallies = jnp.where(number % 4 == 0, named(heavy_load, number // 4), named(ordinary, number - number // 4 - 1))
    mixed = jax.random.permutation(jax.random.fold_in(own, 3), count)
    donor, receiver = mixed[0:count // 2 * 2:2], mixed[1:count // 2 * 2:2]
    room = jnp.minimum(tallies[donor] - 1, bound - tallies[receiver]) // 2
    room = jnp.where((donor == ranking[0]) | (receiver == ranking[0]) | (tallies[receiver] == 0), 0, jnp.maximum(room, 0))
    passed = jax.random.randint(jax.random.fold_in(own, 4), (count // 2,), 0, 1 << 20) % (room + 1)
    tallies = tallies.at[donor].add(-passed).at[receiver].add(passed)
    items = jnp.searchsorted(jnp.cumsum(tallies), jnp.arange(rows * top), side="right").astype(jnp.int32)
    listing = items.reshape(top, rows).T
    listing = listing[jax.random.permutation(jax.random.fold_in(own, 1), rows)]
    rotation = jax.random.randint(jax.random.fold_in(own, 2), (rows, 1), 0, top)
    return jnp.take_along_axis(listing, (jnp.arange(top)[None, :] + rotation) % top, axis=1)


def shares(count, total, most, skew, full):
    portions = [(1 << 20) // math.isqrt(grade ** skew) + 1 for grade in range(1, count + 1)]
    largest = most if full else min(most, max(-(-total // count), total * portions[0] // sum(portions)))
    least = 1 if total - largest >= count - 1 else 0
    counts, spare = [largest] + [least] * (count - 1), total - largest - least * (count - 1)
    while spare > 0:
        candidates = [i for i in range(1, count) if counts[i] < largest] or [i for i in range(1, count) if counts[i] < most]
        whole, remaining = sum([portions[i] for i in candidates]), spare
        for i in candidates:
            extra = min(most - counts[i], max(1, remaining * portions[i] // whole), spare)
            counts[i] = counts[i] + extra
            spare = spare - extra
    return np.array(counts)


def gaussian(stream_key, dims, spread, most, cuts=(), kind=jnp.bfloat16):
    result = jax.random.normal(stream_key, dims, jnp.float32) * spread
    if len(cuts) > 0:
        result = levels(stream_key, dims, cuts, -0.22, 0.18) * result
    return jnp.clip(result, min=-most, max=most).astype(kind)


def setup_inputs(seed: int = 0) -> dict:
    seeds = jax.random.split(jax.random.key(seed), 10)
    a_init = gaussian(seeds[0], (N_PIPE, TOKENS, D), 1.0, 6.0, ((0, 8), (1, 16)))
    b_init = gaussian(seeds[1], (N_PIPE, TOKENS, D), 1.0, 6.0, ((0, 8), (1, 16)))
    incoming = gaussian(seeds[2], (STEPS - 1, TOKENS, D), 1.0, 6.0, ((1, 16),))
    routes_keys = jax.random.split(jax.random.fold_in(seeds[3], 1), N_PIPE * STEPS * 2 * TOKENS // TOK_DEV)
    routes_turns = jax.random.permutation(jax.random.fold_in(seeds[3], 3), N_PIPE * STEPS * 2 * TOKENS // TOK_DEV)
    routes = jax.vmap(lambda own, number: routed_block(jax.random.fold_in(seeds[3], 2), own, number, TOK_DEV, NEXP, TOP, CAP, 2))(routes_keys, routes_turns).reshape((N_PIPE, STEPS, 2, TOKENS, TOP))
    gain = jnp.clip(1.0 + 0.1 * jax.random.normal(seeds[4], (N_PIPE, 2, D), jnp.float32), 0.5, 1.5).astype(jnp.bfloat16)
    router = gaussian(seeds[5], (N_PIPE, 2, D, NEXP), D ** -0.5, 0.09375, ((0, 8),))
    w_gate = gaussian(seeds[6], (N_PIPE, 2, D, NEXP * FF), D ** -0.5, 0.09375, ((0, 8), (3, 16)))
    w_up = gaussian(seeds[7], (N_PIPE, 2, D, NEXP * FF), D ** -0.5, 0.09375, ((0, 8), (3, 16)))
    w_down = gaussian(seeds[8], (N_PIPE, 2, NEXP * FF, D), FF ** -0.5, 0.1875, ((0, 8), (2, 16)))
    return dict(a_init=a_init, b_init=b_init, incoming=incoming, routes=routes, gain=gain, router=router, w_gate=w_gate, w_up=w_up, w_down=w_down)


def apply_layer(state, route_ids, gain_row, router_mat, gate_mat, up_mat, down_mat):
    values = state.astype(jnp.float32)
    mean_square = lax.optimization_barrier(jnp.mean(values * values, axis=-1, keepdims=True))
    normed = (values * lax.rsqrt(mean_square + 1e-06) * gain_row.astype(jnp.float32)).astype(jnp.bfloat16)
    logits = jnp.dot(normed, router_mat, preferred_element_type=jnp.float32)
    chosen = route_ids[:, 0].astype(jnp.int32)
    onehot = (chosen[:, None] == jnp.arange(NEXP, dtype=jnp.int32)[None, :]).astype(jnp.int32)
    weight = 2.5 * jax.nn.sigmoid(lax.optimization_barrier(jnp.sum(logits * onehot.astype(jnp.float32), axis=-1)))
    blocked = onehot.reshape(N_EXPERT, TOK_DEV, NEXP)
    slot_index = lax.optimization_barrier(jnp.sum((jnp.cumsum(blocked, axis=1) - 1) * blocked, axis=-1)).reshape(TOKENS).astype(jnp.int32)
    source = (jnp.arange(TOKENS, dtype=jnp.int32) // TOK_DEV).astype(jnp.int32)
    buffers = jnp.zeros((NEXP, N_EXPERT, CAP, D), jnp.bfloat16).at[chosen, source, slot_index].set(normed)
    gate_split = gate_mat.reshape(D, NEXP, FF).transpose(1, 0, 2)
    up_split = up_mat.reshape(D, NEXP, FF).transpose(1, 0, 2)
    down_split = down_mat.reshape(NEXP, FF, D)

    def one_expert(pieces):
        rows, gate_e, up_e, down_e = pieces
        flat = rows.reshape(N_EXPERT * CAP, D)
        total = jnp.zeros((N_EXPERT * CAP, D), jnp.float32)
        for block in range(SPLIT):
            lower = block * FF_DEV
            gate_val = jnp.dot(flat, gate_e[:, lower:lower + FF_DEV], preferred_element_type=jnp.float32)
            up_val = jnp.dot(flat, up_e[:, lower:lower + FF_DEV], preferred_element_type=jnp.float32)
            hidden = (jax.nn.silu(gate_val) * up_val).astype(jnp.bfloat16)
            partial_value = jnp.dot(hidden, down_e[lower:lower + FF_DEV], preferred_element_type=jnp.float32).astype(jnp.bfloat16)
            partial_value = lax.optimization_barrier(partial_value)
            total = total + partial_value.astype(jnp.float32)
        return total.reshape(N_EXPERT, CAP, D)
    combined = lax.map(one_expert, (buffers, gate_split, up_split, down_split))
    expert_out = combined[chosen, source, slot_index]
    return (values + weight[:, None] * expert_out).astype(jnp.bfloat16)

def reference(a_init, b_init, incoming, routes, gain, router, w_gate, w_up, w_down):
    forward = a_init
    backward = b_init
    outs_a = []
    outs_b = []
    for step_index in range(STEPS):
        layer_fwd = jnp.stack([apply_layer(forward[section], routes[section, step_index, 0], gain[section, 0], router[section, 0], w_gate[section, 0], w_up[section, 0], w_down[section, 0]) for section in range(N_PIPE)])
        layer_bwd = jnp.stack([apply_layer(backward[section], routes[section, step_index, 1], gain[section, 1], router[section, 1], w_gate[section, 1], w_up[section, 1], w_down[section, 1]) for section in range(N_PIPE)])
        outs_a.append(layer_fwd)
        outs_b.append(layer_bwd)
        if step_index + 1 < STEPS:
            forward = jnp.concatenate([incoming[step_index:step_index + 1], layer_fwd[:-1]], axis=0)
            backward = jnp.concatenate([layer_bwd[1:], layer_fwd[-1:]], axis=0)
    return (jnp.stack(outs_a), jnp.stack(outs_b))
```

```python
import functools

import jax
import jax.numpy as jnp
from jax import lax
from jax.experimental import pallas as pl
from jax.experimental.pallas import tpu as pltpu
from jax.sharding import PartitionSpec as P

MESH = pl.DeviceIdType.MESH
F32, BF16, I32 = jnp.float32, jnp.bfloat16, jnp.int32
ROUTE_GAIN = 2.5
SIDE = 4
PARTS = 8
HEAD, TAIL, QUARTERS = 16, 4, 4
WINDOW = 3


def iota(shape, axis):
    return lax.broadcasted_iota(I32, shape, axis)


def ones_where(mask):
    return jnp.where(mask, 1.0, 0.0).astype(BF16)


def dot(left, right):
    return jnp.dot(left, right, preferred_element_type=F32)


def relay(
    pipe_count,
    a_in, b_in, later_in, routes, gain, router, gate_in, up_in, down_in,
    a_out, b_out,
    gate, up, down, own_x, near_x, near_routes, normed, packed, got, part, crossed, returned, outs, rows, hidden, tail_rows,
    spread, weight,
    load_sem, gate_sem, store_sem, route_send, route_recv, x_send, x_recv, chunk_send, chunk_recv, cross_send, cross_recv,
    back_send, back_recv, pipe_send, pipe_recv,
):
    tokens, width = own_x.shape[2:]
    quarter = width // QUARTERS
    block = PARTS * HEAD
    tails = PARTS * TAIL
    pipe, place = lax.axis_index("pipe"), lax.axis_index("expert")
    y, x = place // SIDE, place % SIDE
    near = y * SIDE + x + 1 - 2 * (x % 2)
    inputs, results = (a_in, b_in), (a_out, b_out)

    def columns(q):
        return slice(q * quarter, (q + 1) * quarter)

    def partner(k, way):
        column = x + (k // SIDE) * (SIDE - 1 - 2 * x)
        return ((y + SIDE + way * (k % SIDE)) % SIDE) * SIDE + column

    def piece(k):
        if isinstance(k, int):
            return pl.ds(k * HEAD, HEAD)
        return pl.ds(pl.multiple_of(k * HEAD, HEAD), HEAD)

    def remote(source, target, send, recv, device):
        return pltpu.make_async_remote_copy(
            src_ref=source, dst_ref=target, send_sem=send, recv_sem=recv, device_id=device, device_id_type=MESH
        )

    def chunk_copy(g, h, k):
        return remote(
            packed.at[g, h, piece(k)], got.at[g, h, piece(k)], chunk_send.at[g, h, k], chunk_recv.at[g, h, k],
            (pipe, partner(k, 1)),
        )

    def back_copy(g, k):
        return remote(
            part.at[g, 0, piece(k)], returned.at[g, piece(k)], back_send.at[g, k], back_recv.at[g, k],
            (pipe, partner(k, -1)),
        )

    def cross_copy(g, k):
        return remote(
            part.at[g, 1, piece(k)], crossed.at[g, piece(k)], cross_send.at[g, k], cross_recv.at[g, k], (pipe, near)
        )

    def x_copy(s, g):
        source = inputs[g].at[0] if s == 0 else own_x.at[s, g]
        return remote(source, near_x.at[s, g], x_send.at[g], x_recv.at[g], (pipe, near))

    def route_copy():
        return remote(routes, near_routes, route_send, route_recv, (pipe, near))

    def pipe_copy(g):
        return remote(outs.at[g], own_x.at[1, g], pipe_send.at[g], pipe_recv.at[g], (pipe + 1 - 2 * g, place))

    def has_next(g):
        return pipe < pipe_count - 1 if g == 0 else pipe > 0

    def load_copy(g):
        return pltpu.make_async_copy(inputs[g].at[0], own_x.at[0, g], load_sem.at[g])

    def weight_copies(g):
        return [
            pltpu.make_async_copy(source.at[0, g], target.at[g], gate_sem.at[g, i])
            for i, (source, target) in enumerate(((gate_in, gate), (up_in, up), (down_in, down)))
        ]

    def store_copy(s, g):
        return pltpu.make_async_copy(outs.at[g], results[g].at[s, 0], store_sem.at[g])

    def later_copy():
        return pltpu.make_async_copy(later_in.at[0], own_x.at[1, 0], pipe_recv.at[0])

    def turn_copy():
        return pltpu.make_async_copy(outs.at[0], own_x.at[1, 1], pipe_recv.at[1])

    def each(first, last, action):
        lax.fori_loop(first, last, lambda k, carry: (action(k), carry)[1], 0)

    def slot_codes(chosen):
        hot = iota((PARTS, tokens), 0) == chosen
        upper = ones_where(iota((tokens, tokens), 0) <= iota((tokens, tokens), 1))
        seen = dot(ones_where(hot), upper)
        slot = jnp.sum(jnp.where(hot, seen - 1.0, 0.0), axis=0, keepdims=True)
        return chosen * 32 + slot.astype(I32)

    def selectors(codes, axis):
        shape = (block, tokens) if axis == 0 else (tokens, block)
        row = iota(shape, axis)
        k, low = row // HEAD, row % HEAD
        expert = 2 * ((y + k) % SIDE) + jnp.where(k >= SIDE, SIDE - 1 - x, x) // 2
        head = ones_where(codes == expert * 32 + low)
        tail_hit = codes == expert * 32 + HEAD + low % TAIL
        return head, [ones_where(tail_hit & (low // TAIL == q)) for q in range(QUARTERS)]

    def prepare(s, g, h):
        source = (own_x if h == 0 else near_x).at[s, g]
        gains = gain[...].astype(F32)[g:g + 1]

        def normalize(i):
            at = pl.multiple_of(i * HEAD, HEAD)
            values = source[pl.ds(at, HEAD), :].astype(F32)
            mean_square = jnp.mean(values * values, axis=-1, keepdims=True)
            scaled = (values * lax.rsqrt(mean_square + 1e-06) * gains).astype(BF16)
            for q in range(QUARTERS):
                normed[q, pl.ds(at, HEAD), :] = scaled[:, columns(q)]

        each(0, tokens // HEAD, normalize)
        chosen = (routes if h == 0 else near_routes)[2 * s + g:2 * s + g + 1, :]
        codes = slot_codes(chosen)
        head, tail = selectors(codes, 0)
        for q in range(QUARTERS):
            packed[g, h, :, columns(q)] = dot(head, normed[q]).astype(BF16)
        total = dot(tail[0], normed[0])
        for q in range(1, QUARTERS):
            total = total + dot(tail[q], normed[q])
        packed[g, h, :, width:] = total.astype(BF16)
        if h == 0:
            codes_down = jnp.transpose(jnp.broadcast_to(codes.astype(F32), (tokens, tokens))).astype(I32)
            head_down, tail_down = selectors(codes_down, 1)
            spread[g, 0] = head_down
            for q in range(QUARTERS):
                spread[g, 1 + q] = tail_down[q]
            logits = jnp.zeros((tokens, PARTS), F32)
            for q in range(QUARTERS):
                logits = logits + lax.dot_general(
                    normed[q], router[g, :, columns(q)], (((1,), (1,)), ((), ())), preferred_element_type=F32
                )
            mine = iota((tokens, PARTS), 1) == codes_down[:, :PARTS] // 32
            logit = jnp.sum(jnp.where(mine, logits, 0.0), axis=-1, keepdims=True)
            weight[g] = jnp.broadcast_to(ROUTE_GAIN * jax.nn.sigmoid(logit), (tokens, 128))

    def send_chunks(g, h):
        got[g, h, 0:HEAD, :] = packed[g, h, 0:HEAD, :]
        each(1, PARTS, lambda k: chunk_copy(g, h, k).start())

    def wait_chunks(g, h):
        each(1, PARTS, lambda k: chunk_copy(g, h, k).wait())

    def expert(g, h):
        out_row, in_row = iota((block, block), 0), iota((block, block), 1)
        gather = (out_row // TAIL % PARTS) * HEAD + (out_row // tails) * TAIL + out_row % TAIL
        scatter = (out_row % HEAD // TAIL) * tails + (out_row // HEAD) * TAIL + out_row % TAIL
        rows[0:block, :] = got[g, h, :, 0:width]
        tail = dot(ones_where(in_row == gather), got[g, h, :, width:]).astype(BF16)
        for q in range(QUARTERS):
            rows[block:, columns(q)] = tail[q * tails:(q + 1) * tails]
        units = hidden.shape[1]
        inner = min(256, units)

        def widen(j):
            at = pl.ds(pl.multiple_of(j * inner, inner), inner)
            gate_val = dot(rows[...], gate[g, :, at])
            up_val = dot(rows[...], up[g, :, at])
            hidden[:, at] = (gate_val * jax.nn.sigmoid(gate_val) * up_val).astype(BF16)

        each(0, units // inner, widen)
        step = min(512, width)

        def narrow(j):
            at = pl.ds(pl.multiple_of(j * step, step), step)
            value = dot(hidden[...], down[g, :, at]).astype(BF16)
            part[g, h, :, at] = value[:block]
            tail_rows[:, at] = value[block:]

        each(0, width // step, narrow)
        stacked = jnp.concatenate([tail_rows[:, columns(q)] for q in range(QUARTERS)], axis=0)
        part[g, h, :, width:] = dot(ones_where(in_row == scatter), stacked).astype(BF16)

    def start_cross(g):
        each(0, WINDOW, lambda k: cross_copy(g, k).start())

    def finish_cross(g, first, last):
        def one(k):
            cross_copy(g, k).wait_recv()

            @pl.when(k + WINDOW < PARTS)
            def _():
                cross_copy(g, k + WINDOW).start()

            for q in range(QUARTERS + 1):
                at = columns(q)
                total = part[g, 0, piece(k), at].astype(F32) + crossed[g, piece(k), at].astype(F32)
                part[g, 0, piece(k), at] = total.astype(BF16)

            @pl.when(k > 0)
            def _():
                back_copy(g, k).start()

            @pl.when(k == 0)
            def _():
                returned[g, 0:HEAD, :] = part[g, 0, 0:HEAD, :]

        each(first, last, one)

    def end_cross(g):
        each(0, PARTS, lambda k: cross_copy(g, k).wait_send())

    def combine(s, g):
        each(1, PARTS, lambda k: back_copy(g, k).wait())
        if s == 1:
            store_copy(0, g).wait()
            pl.when(has_next(g))(lambda: pipe_copy(g).wait_send())
        for q in range(QUARTERS):
            at = columns(q)
            expert_out = dot(spread[g, 0], returned[g, :, at]) + dot(spread[g, 1 + q], returned[g, :, width:])
            values = own_x[s, g, :, at].astype(F32)
            outs[g, :, at] = (values + weight[g, :, 0:1] * expert_out).astype(BF16)
        if s == 0:
            pl.when(has_next(g))(lambda: pipe_copy(g).start())
            if g == 0:
                pl.when(pipe == pipe_count - 1)(lambda: turn_copy().start())
        store_copy(s, g).start()

    def wait_pipe(g):
        pltpu.make_async_copy(outs.at[g], own_x.at[1, g], pipe_recv.at[g]).wait()

    for g in (0, 1):
        load_copy(g).start()
    for g in (0, 1):
        for copy in weight_copies(g):
            copy.start()
    pl.when(pipe == 0)(lambda: later_copy().start())

    barrier = pltpu.get_barrier_semaphore()

    def greet(device):
        pl.semaphore_signal(barrier, inc=1, device_id=device, device_id_type=MESH)

    each(1, PARTS, lambda k: greet((pipe, partner(k, 1))))
    greet((pipe, near))
    pl.when(pipe > 0)(lambda: greet((pipe - 1, place)))
    pl.when(pipe < pipe_count - 1)(lambda: greet((pipe + 1, place)))
    before, after = (pipe + pipe_count - 1) // pipe_count, (2 * pipe_count - 2 - pipe) // pipe_count
    pl.semaphore_wait(barrier, PARTS + before + after)

    route_copy().start()
    x_copy(0, 0).start()
    load_copy(0).wait()
    prepare(0, 0, 0)
    send_chunks(0, 0)
    load_copy(1).wait()
    prepare(0, 1, 0)
    wait_chunks(0, 0)
    send_chunks(1, 0)
    for g in (0, 1):
        for copy in weight_copies(g):
            copy.wait()
    expert(0, 0)
    route_copy().wait()

    for s in (0, 1):
        x_copy(s, 0).wait()
        x_copy(s, 1).start()
        prepare(s, 0, 1)
        send_chunks(0, 1)
        wait_chunks(1, 0)
        expert(1, 0)
        wait_chunks(0, 1)
        expert(0, 1)
        x_copy(s, 1).wait()
        start_cross(0)
        prepare(s, 1, 1)
        send_chunks(1, 1)
        finish_cross(0, 0, 4)
        wait_chunks(1, 1)
        expert(1, 1)
        finish_cross(0, 4, PARTS)
        end_cross(0)
        start_cross(1)
        combine(s, 0)
        finish_cross(1, 0, 4)
        if s == 0:
            wait_pipe(0)
            prepare(1, 0, 0)
            send_chunks(0, 0)
        finish_cross(1, 4, PARTS)
        end_cross(1)
        if s == 0:
            x_copy(1, 0).start()
        combine(s, 1)
        if s == 0:
            wait_chunks(0, 0)
            expert(0, 0)
            wait_pipe(1)
            prepare(1, 1, 0)
            send_chunks(1, 0)
    for g in (0, 1):
        store_copy(1, g).wait()


def solution(mesh):
    pipe_count = mesh.shape["pipe"]

    def body(a_init, b_init, incoming, routes, gain, router, w_gate, w_up, w_down):
        tokens, width = a_init.shape[1:]
        units = w_gate.shape[-1]
        quarter = width // QUARTERS
        long = width + quarter
        block = PARTS * HEAD
        steps = routes.shape[1]
        chosen = jnp.pad(routes.reshape(steps * 2, tokens), ((0, 8 - steps * 2), (0, 0)))
        whole = pl.BlockSpec(memory_space=pltpu.VMEM)
        outside = pl.BlockSpec(memory_space=pl.ANY)
        result = jax.ShapeDtypeStruct((steps, 1, tokens, width), BF16)
        dma = pltpu.SemaphoreType.DMA
        return pl.pallas_call(
            functools.partial(relay, pipe_count),
            out_shape=(result, result),
            in_specs=[outside] * 3 + [whole] * 3 + [outside] * 3,
            out_specs=(outside, outside),
            scratch_shapes=[
                pltpu.VMEM((2, width, units), BF16),
                pltpu.VMEM((2, width, units), BF16),
                pltpu.VMEM((2, units, width), BF16),
                pltpu.VMEM((2, 2, tokens, width), BF16),
                pltpu.VMEM((2, 2, tokens, width), BF16),
                pltpu.VMEM((8, tokens), I32),
                pltpu.VMEM((QUARTERS, tokens, quarter), BF16),
                pltpu.VMEM((2, 2, block, long), BF16),
                pltpu.VMEM((2, 2, block, long), BF16),
                pltpu.VMEM((2, 2, block, long), BF16),
                pltpu.VMEM((2, block, long), BF16),
                pltpu.VMEM((2, block, long), BF16),
                pltpu.VMEM((2, tokens, width), BF16),
                pltpu.VMEM((block + PARTS * TAIL, width), BF16),
                pltpu.VMEM((block + PARTS * TAIL, units), BF16),
                pltpu.VMEM((PARTS * TAIL, width), BF16),
                pltpu.VMEM((2, 1 + QUARTERS, tokens, block), BF16),
                pltpu.VMEM((2, tokens, 128), F32),
                dma((2,)),
                dma((2, 3)),
                dma((2,)),
                dma,
                dma,
                dma((2,)),
                dma((2,)),
                dma((2, 2, PARTS)),
                dma((2, 2, PARTS)),
                dma((2, PARTS)),
                dma((2, PARTS)),
                dma((2, PARTS)),
                dma((2, PARTS)),
                dma((2,)),
                dma((2,)),
            ],
            compiler_params=pltpu.CompilerParams(
                collective_id=0, has_side_effects=True, vmem_limit_bytes=63 * 2**20
            ),
            cost_estimate=pl.CostEstimate(
                flops=4 * 320 * width * units * 6, bytes_accessed=6 * width * units * 2 * 2, transcendentals=0
            ),
        )(a_init, b_init, incoming, chosen, gain[0], jnp.swapaxes(router[0], 1, 2), w_gate, w_up, w_down)

    placed = (
        P("pipe", "expert", None),
        P("pipe", "expert", None),
        P(None, "expert", None),
        P("pipe", None, None, "expert", None),
        P("pipe", None, None),
        P("pipe", None, None, None),
        P("pipe", None, None, "expert"),
        P("pipe", None, None, "expert"),
        P("pipe", None, "expert", None),
    )
    return jax.shard_map(
        body,
        mesh=mesh,
        in_specs=placed,
        out_specs=(P(None, "pipe", "expert", None), P(None, "pipe", "expert", None)),
        check_vma=False,
    )
```

```python
import functools

import jax
import jax.numpy as jnp
from jax import lax
from jax.experimental import pallas as pl
from jax.experimental.pallas import tpu as pltpu
from jax.sharding import PartitionSpec as P

MESH = pl.DeviceIdType.MESH
F32, BF16, I32 = jnp.float32, jnp.bfloat16, jnp.int32
ROUTE_GAIN = 2.5
SIDE = 4
PARTS = 8
HEAD, TAIL = 16, 4
LANES, CELLS = 128, 4
TILE, LONG = CELLS * LANES, CELLS * LANES + LANES


def pieces_of(width):
    tiles = width // TILE
    cuts = list(range(0, tiles, 2 if tiles > 4 else 1)) + [tiles]
    return list(zip(cuts[:-1], cuts[1:]))


def iota(shape, axis):
    return lax.broadcasted_iota(I32, shape, axis)


def ones_where(mask):
    return jnp.where(mask, 1.0, 0.0).astype(BF16)


def dot(left, right):
    return jnp.dot(left, right, preferred_element_type=F32)


ORDER = (
    ("select", 0, 0, 0), ("select", 0, 0, 1), ("weigh", 0, 0), ("own", 0, 0, 0), ("near", 0, 0, 0), ("own", 0, 0, 1),
    ("near", 0, 0, 1), ("select", 0, 1, 0), ("select", 0, 1, 1), ("near", 0, 0, 2), ("own", 0, 0, 2), ("near", 0, 0, 3),
    ("near", 0, 1, 0), ("own", 0, 1, 0), ("own", 0, 0, 3), ("expert", 0, 0, 1), ("near", 0, 1, 1), ("expert", 0, 0, 0),
    ("near", 0, 1, 2), ("finish", 0, 0, 0), ("near", 0, 1, 3), ("finish", 0, 0, 1), ("own", 0, 1, 1), ("expert", 0, 1, 1),
    ("finish", 0, 0, 2), ("combine", 0, 0, 0), ("combine", 0, 0, 1), ("own", 0, 1, 2), ("finish", 0, 0, 3), ("own", 0, 1, 3),
    ("combine", 0, 0, 2), ("combine", 0, 0, 3), ("take", 1, 0, 0), ("take", 1, 0, 1), ("select", 1, 0, 0), ("own", 1, 0, 0),
    ("weigh", 0, 1), ("own", 1, 0, 1), ("expert", 0, 1, 0), ("take", 1, 0, 2), ("take", 1, 0, 3), ("finish", 0, 1, 0),
    ("finish", 0, 1, 1), ("combine", 0, 1, 0), ("own", 1, 0, 2), ("finish", 0, 1, 2), ("select", 1, 0, 1),
    ("combine", 0, 1, 1), ("finish", 0, 1, 3), ("own", 1, 0, 3), ("near", 1, 0, 0), ("combine", 0, 1, 2), ("weigh", 1, 0),
    ("near", 1, 0, 1), ("combine", 0, 1, 3), ("take", 1, 1, 0), ("take", 1, 1, 1), ("select", 1, 1, 0), ("take", 1, 1, 2),
    ("take", 1, 1, 3), ("near", 1, 0, 2), ("own", 1, 1, 0), ("select", 1, 1, 1), ("near", 1, 0, 3), ("own", 1, 1, 1),
    ("own", 1, 1, 2), ("own", 1, 1, 3), ("expert", 1, 0, 0), ("near", 1, 1, 0), ("near", 1, 1, 1), ("expert", 1, 0, 1),
    ("expert", 1, 1, 0), ("near", 1, 1, 2), ("near", 1, 1, 3), ("finish", 1, 0, 0), ("weigh", 1, 1), ("finish", 1, 0, 1),
    ("expert", 1, 1, 1), ("finish", 1, 1, 0), ("finish", 1, 0, 2), ("finish", 1, 1, 1), ("finish", 1, 0, 3),
    ("combine", 1, 0, 0), ("combine", 1, 0, 1), ("combine", 1, 1, 0), ("combine", 1, 0, 2), ("finish", 1, 1, 2),
    ("combine", 1, 1, 1), ("finish", 1, 1, 3), ("combine", 1, 1, 2), ("combine", 1, 0, 3), ("combine", 1, 1, 3),
)


def relay(
    pipe_count,
    a_in, b_in, later_in, routes, gain, router, gate_in, up_in, down_in,
    a_out, b_out,
    gate, up, down, own_x, near_x, near_routes, normed, packed, got, part, crossed, returned, outs, rows, hidden,
    pick, spread, placed_at, weight,
    load_sem, weight_sem, store_sem, route_send, route_recv, x_send, x_recv, chunk_send, chunk_recv, cross_send, cross_recv,
    back_send, back_recv, pipe_send, pipe_recv,
):
    tokens, width = own_x.shape[2:]
    block = PARTS * HEAD
    tails = PARTS * TAIL
    tiles = width // TILE
    pieces = pieces_of(width)
    every = range(len(pieces))
    loaded = set()
    pipe, place = lax.axis_index("pipe"), lax.axis_index("expert")
    y, x = place // SIDE, place % SIDE
    near = y * SIDE + x + 1 - 2 * (x % 2)
    inputs, results = (a_in, b_in), (a_out, b_out)

    def plain(p):
        return slice(pieces[p][0] * TILE, pieces[p][1] * TILE)

    def wide(p):
        return slice(pieces[p][0] * LONG, pieces[p][1] * LONG)

    def partner(k, way):
        column = x + (k // SIDE) * (SIDE - 1 - 2 * x)
        return ((y + SIDE + way * (k % SIDE)) % SIDE) * SIDE + column

    def chunk(k):
        return pl.ds(pl.multiple_of(k * HEAD, HEAD), HEAD)

    def remote(source, target, send, recv, device):
        return pltpu.make_async_remote_copy(
            src_ref=source, dst_ref=target, send_sem=send, recv_sem=recv, device_id=device, device_id_type=MESH
        )

    def chunk_copy(g, h, p, k):
        return remote(
            packed.at[g, h, chunk(k), wide(p)], got.at[g, h, chunk(k), wide(p)],
            chunk_send.at[g, h, p, k], chunk_recv.at[g, h, p, k], (pipe, partner(k, 1)),
        )

    def back_copy(g, p, k):
        return remote(
            part.at[g, 0, chunk(k), wide(p)], returned.at[g, chunk(k), wide(p)],
            back_send.at[g, p, k], back_recv.at[g, p, k], (pipe, partner(k, -1)),
        )

    def cross_copy(g, p):
        return remote(
            part.at[g, 1, :, wide(p)], crossed.at[g, :, wide(p)], cross_send.at[g, p], cross_recv.at[g, p], (pipe, near)
        )

    def x_copy(s, g, p):
        source = inputs[g].at[0, :, plain(p)] if s == 0 else own_x.at[s, g, :, plain(p)]
        return remote(source, near_x.at[s, g, :, plain(p)], x_send.at[g, p], x_recv.at[g, p], (pipe, near))

    def route_copy():
        return remote(routes, near_routes, route_send, route_recv, (pipe, near))

    def pipe_copy(g, p):
        return remote(
            outs.at[g, :, plain(p)], own_x.at[1, g, :, plain(p)], pipe_send.at[g, p], pipe_recv.at[g, p],
            (pipe + 1 - 2 * g, place),
        )

    def has_next(g):
        return pipe < pipe_count - 1 if g == 0 else pipe > 0

    def load_copy(g):
        return pltpu.make_async_copy(inputs[g].at[0], own_x.at[0, g], load_sem.at[g])

    def weight_copies(g):
        return [
            pltpu.make_async_copy(source.at[0, g], target.at[g], weight_sem.at[g, i])
            for i, (source, target) in enumerate(((gate_in, gate), (up_in, up), (down_in, down)))
        ]

    def store_copy(s, g, p):
        return pltpu.make_async_copy(outs.at[g, :, plain(p)], results[g].at[s, 0, :, plain(p)], store_sem.at[g, p])

    def later_copy(p):
        return pltpu.make_async_copy(later_in.at[0, :, plain(p)], own_x.at[1, 0, :, plain(p)], pipe_recv.at[0, p])

    def turn_copy(p):
        return pltpu.make_async_copy(outs.at[0, :, plain(p)], own_x.at[1, 1, :, plain(p)], pipe_recv.at[1, p])

    def each(first, last, action):
        lax.fori_loop(first, last, lambda k, carry: (action(k), carry)[1], 0)

    def slot_codes(chosen):
        hot = iota((PARTS, tokens), 0) == chosen
        upper = ones_where(iota((tokens, tokens), 0) <= iota((tokens, tokens), 1))
        seen = dot(ones_where(hot), upper)
        slot = jnp.sum(jnp.where(hot, seen - 1.0, 0.0), axis=0, keepdims=True)
        return chosen * 32 + slot.astype(I32)

    def selectors(codes, axis):
        shape = (block, tokens) if axis == 0 else (tokens, block)
        row = iota(shape, axis)
        k, low = row // HEAD, row % HEAD
        expert = 2 * ((y + k) % SIDE) + jnp.where(k >= SIDE, SIDE - 1 - x, x) // 2
        tail_hit = codes == expert * 32 + HEAD + low % TAIL
        return [ones_where(codes == expert * 32 + low)] + [ones_where(tail_hit & (low // TAIL == b)) for b in range(CELLS)]

    def select(s, g, h):
        chosen = (routes if h == 0 else near_routes)[2 * s + g:2 * s + g + 1, :]
        codes = slot_codes(chosen)
        for i, selector in enumerate(selectors(codes, 0)):
            pick[g, h, i] = selector
        if h == 0:
            codes_down = jnp.transpose(jnp.broadcast_to(codes.astype(F32), (tokens, tokens))).astype(I32)
            placed_at[g] = codes_down
            for i, selector in enumerate(selectors(codes_down, 1)):
                spread[g, i] = selector

    def normalize(source, target, gains, count):
        def one(i):
            at = pl.ds(pl.multiple_of(i * HEAD, HEAD), HEAD)
            values = source[at, :].astype(F32)
            mean_square = jnp.mean(values * values, axis=-1, keepdims=True)
            target[at, :] = (values * lax.rsqrt(mean_square + 1e-06) * gains).astype(BF16)

        each(0, count // HEAD, one)

    def weigh(s, g):
        normalize(own_x.at[s, g], normed, gain[...].astype(F32)[g:g + 1], tokens)
        logits = lax.dot_general(normed[...], router[g], (((1,), (1,)), ((), ())), preferred_element_type=F32)
        mine = iota((tokens, PARTS), 1) == placed_at[g, :, 0:PARTS] // 32
        logit = jnp.sum(jnp.where(mine, logits, 0.0), axis=-1, keepdims=True)
        weight[g] = jnp.broadcast_to(ROUTE_GAIN * jax.nn.sigmoid(logit), (tokens, LANES))

    def send_piece(s, g, h, p):
        source = (own_x if h == 0 else near_x).at[s, g]
        for c in range(*pieces[p]):
            values = source[:, c * TILE:(c + 1) * TILE]
            packed[g, h, :, c * LONG:c * LONG + TILE] = dot(pick[g, h, 0], values).astype(BF16)
            total = dot(pick[g, h, 1], values[:, :LANES])
            for b in range(1, CELLS):
                total = total + dot(pick[g, h, 1 + b], values[:, b * LANES:(b + 1) * LANES])
            packed[g, h, :, c * LONG + TILE:(c + 1) * LONG] = total.astype(BF16)
        each(1, PARTS, lambda k: chunk_copy(g, h, p, k).start())
        got[g, h, 0:HEAD, wide(p)] = packed[g, h, 0:HEAD, wide(p)]

    def send_own(s, g, p):
        send_piece(s, g, 0, p)

    def send_near(s, g, p):
        x_copy(s, g, p).wait()
        send_piece(s, g, 1, p)

    def wait_chunks(g, h):
        for p in every:
            each(1, PARTS, lambda k: chunk_copy(g, h, p, k).wait())

    def expert(s, g, h):
        if g not in loaded:
            loaded.add(g)
            for copy in weight_copies(g):
                copy.wait()
        wait_chunks(g, h)
        out_row, in_row = iota((block, block), 0), iota((block, block), 1)
        gather = (out_row // TAIL % PARTS) * HEAD + (out_row // tails) * TAIL + out_row % TAIL
        scatter = ones_where(in_row == (out_row % HEAD // TAIL) * tails + (out_row // HEAD) * TAIL + out_row % TAIL)
        for c in range(tiles):
            rows[0:block, c * TILE:(c + 1) * TILE] = got[g, h, :, c * LONG:c * LONG + TILE]
        cells = jnp.concatenate([got[g, h, :, c * LONG + TILE:(c + 1) * LONG] for c in range(tiles)], axis=1)
        cells = dot(ones_where(in_row == gather), cells).astype(BF16)
        for c in range(tiles):
            for b in range(CELLS):
                at = c * TILE + b * LANES
                rows[block:, at:at + LANES] = cells[b * tails:(b + 1) * tails, c * LANES:(c + 1) * LANES]
        normalize(rows, rows, gain[...].astype(F32)[g:g + 1], block + tails)
        units = hidden.shape[1]
        inner = min(256, units)

        def widen(j):
            at = pl.ds(pl.multiple_of(j * inner, inner), inner)
            gate_val = dot(rows[...], gate[g, :, at])
            up_val = dot(rows[...], up[g, :, at])
            hidden[:, at] = (gate_val * jax.nn.sigmoid(gate_val) * up_val).astype(BF16)

        each(0, units // inner, widen)

        def narrow(c):
            value = dot(hidden[...], down[g, :, pl.ds(pl.multiple_of(c * TILE, TILE), TILE)]).astype(BF16)
            part[g, h, :, pl.ds(pl.multiple_of(c * LONG, LANES), TILE)] = value[:block]
            stacked = jnp.concatenate([value[block:, b * LANES:(b + 1) * LANES] for b in range(CELLS)], axis=0)
            part[g, h, :, pl.ds(pl.multiple_of(c * LONG + TILE, LANES), LANES)] = dot(scatter, stacked).astype(BF16)

        for p in every:
            each(*pieces[p], narrow)
            if h == 1:
                cross_copy(g, p).start()

    def finish_cross(s, g, p):
        cross_copy(g, p).wait()
        for c in range(*pieces[p]):
            at = slice(c * LONG, (c + 1) * LONG)
            part[g, 0, :, at] = (part[g, 0, :, at].astype(F32) + crossed[g, :, at].astype(F32)).astype(BF16)
        each(1, PARTS, lambda k: back_copy(g, p, k).start())
        returned[g, 0:HEAD, wide(p)] = part[g, 0, 0:HEAD, wide(p)]

    def combine(s, g, p):
        each(1, PARTS, lambda k: back_copy(g, p, k).wait())
        if s == 1:
            store_copy(0, g, p).wait()
            pl.when(has_next(g))(lambda: pipe_copy(g, p).wait_send())
        for c in range(*pieces[p]):
            at = slice(c * TILE, (c + 1) * TILE)
            cells = returned[g, :, c * LONG + TILE:(c + 1) * LONG]
            expert_out = dot(spread[g, 0], returned[g, :, c * LONG:c * LONG + TILE])
            expert_out = expert_out + jnp.concatenate([dot(spread[g, 1 + b], cells) for b in range(CELLS)], axis=1)
            values = own_x[s, g, :, at].astype(F32)
            outs[g, :, at] = (values + weight[g, :, 0:1] * expert_out).astype(BF16)
        if s == 0:
            pl.when(has_next(g))(lambda: pipe_copy(g, p).start())
            if g == 0:
                pl.when(pipe == pipe_count - 1)(lambda: turn_copy(p).start())
        store_copy(s, g, p).start()

    def take(s, g, p):
        pltpu.make_async_copy(outs.at[g, :, plain(p)], own_x.at[s, g, :, plain(p)], pipe_recv.at[g, p]).wait()
        x_copy(s, g, p).start()

    for g in (0, 1):
        load_copy(g).start()
    for g in (0, 1):
        for copy in weight_copies(g):
            copy.start()

    @pl.when(pipe == 0)
    def _():
        for p in every:
            later_copy(p).start()

    barrier = pltpu.get_barrier_semaphore()

    def greet(device):
        pl.semaphore_signal(barrier, inc=1, device_id=device, device_id_type=MESH)

    each(1, PARTS, lambda k: greet((pipe, partner(k, 1))))
    greet((pipe, near))
    pl.when(pipe > 0)(lambda: greet((pipe - 1, place)))
    pl.when(pipe < pipe_count - 1)(lambda: greet((pipe + 1, place)))
    before, after = (pipe + pipe_count - 1) // pipe_count, (2 * pipe_count - 2 - pipe) // pipe_count
    pl.semaphore_wait(barrier, PARTS + before + after)

    route_copy().start()
    for g in (0, 1):
        for p in every:
            x_copy(0, g, p).start()
    route_copy().wait()
    for g in (0, 1):
        load_copy(g).wait()
    actions = dict(
        select=select, own=send_own, near=send_near, take=take, weigh=weigh, expert=expert, finish=finish_cross, combine=combine
    )
    for name, *where in ORDER:
        actions[name](*where)
    for g in (0, 1):
        for p in every:
            store_copy(1, g, p).wait()


def solution(mesh):
    pipe_count = mesh.shape["pipe"]

    def body(a_init, b_init, incoming, routes, gain, router, w_gate, w_up, w_down):
        tokens, width = a_init.shape[1:]
        units = w_gate.shape[-1]
        long = width // TILE * LONG
        block = PARTS * HEAD
        count = len(pieces_of(width))
        steps = routes.shape[1]
        chosen = routes.reshape(steps * 2, tokens)
        whole = pl.BlockSpec(memory_space=pltpu.VMEM)
        outside = pl.BlockSpec(memory_space=pl.ANY)
        result = jax.ShapeDtypeStruct((steps, 1, tokens, width), BF16)
        dma = pltpu.SemaphoreType.DMA
        return pl.pallas_call(
            functools.partial(relay, pipe_count),
            out_shape=(result, result),
            in_specs=[outside] * 3 + [whole] * 3 + [outside] * 3,
            out_specs=(outside, outside),
            scratch_shapes=[
                pltpu.VMEM((2, width, units), BF16),
                pltpu.VMEM((2, width, units), BF16),
                pltpu.VMEM((2, units, width), BF16),
                pltpu.VMEM((2, 2, tokens, width), BF16),
                pltpu.VMEM((2, 2, tokens, width), BF16),
                pltpu.VMEM((steps * 2, tokens), I32),
                pltpu.VMEM((tokens, width), BF16),
                pltpu.VMEM((2, 2, block, long), BF16),
                pltpu.VMEM((2, 2, block, long), BF16),
                pltpu.VMEM((2, 2, block, long), BF16),
                pltpu.VMEM((2, block, long), BF16),
                pltpu.VMEM((2, block, long), BF16),
                pltpu.VMEM((2, tokens, width), BF16),
                pltpu.VMEM((block + PARTS * TAIL, width), BF16),
                pltpu.VMEM((block + PARTS * TAIL, units), BF16),
                pltpu.VMEM((2, 2, 1 + CELLS, block, tokens), BF16),
                pltpu.VMEM((2, 1 + CELLS, tokens, block), BF16),
                pltpu.VMEM((2, tokens, tokens), I32),
                pltpu.VMEM((2, tokens, LANES), F32),
                dma((2,)),
                dma((2, 3)),
                dma((2, count)),
                dma,
                dma,
                dma((2, count)),
                dma((2, count)),
                dma((2, 2, count, PARTS)),
                dma((2, 2, count, PARTS)),
                dma((2, count)),
                dma((2, count)),
                dma((2, count, PARTS)),
                dma((2, count, PARTS)),
                dma((2, count)),
                dma((2, count)),
            ],
            compiler_params=pltpu.CompilerParams(
                collective_id=0, has_side_effects=True, vmem_limit_bytes=63 * 2**20
            ),
            cost_estimate=pl.CostEstimate(
                flops=4 * 320 * width * units * 6, bytes_accessed=6 * width * units * 2 * 2, transcendentals=0
            ),
        )(a_init, b_init, incoming, chosen, gain[0], jnp.swapaxes(router[0], 1, 2), w_gate, w_up, w_down)

    placed = (
        P("pipe", "expert", None),
        P("pipe", "expert", None),
        P(None, "expert", None),
        P("pipe", None, None, "expert", None),
        P("pipe", None, None),
        P("pipe", None, None, None),
        P("pipe", None, None, "expert"),
        P("pipe", None, None, "expert"),
        P("pipe", None, "expert", None),
    )
    return jax.shard_map(
        body,
        mesh=mesh,
        in_specs=placed,
        out_specs=(P(None, "pipe", "expert", None), P(None, "pipe", "expert", None)),
        check_vma=False,
    )
```

```python
import functools

import jax
import jax.numpy as jnp
from jax import lax
from jax.experimental import pallas as pl
from jax.experimental.pallas import tpu as pltpu
from jax.sharding import PartitionSpec as P

MESH = pl.DeviceIdType.MESH
F32, BF16, I32 = jnp.float32, jnp.bfloat16, jnp.int32
ROUTE_GAIN = 2.5
SIDE = 4
PARTS = 8
HEAD, TAIL = 16, 4
LANES, CELLS = 128, 4
TILE, LONG = CELLS * LANES, CELLS * LANES + LANES


def pieces_of(width):
    tiles = width // TILE
    cuts = list(range(0, tiles, 2 if tiles > 4 else 1)) + [tiles]
    return list(zip(cuts[:-1], cuts[1:]))


DIRECT = 2


def iota(shape, axis):
    return lax.broadcasted_iota(I32, shape, axis)


def ones_where(mask):
    return jnp.where(mask, 1.0, 0.0).astype(BF16)


def dot(left, right):
    return jnp.dot(left, right, preferred_element_type=F32)


ORDER = (
    ("select", 0, 1, 0), ("own", 0, 1, 0), ("select", 0, 0, 0), ("own", 0, 0, 0), ("select", 0, 0, 1), ("own", 0, 0, 1),
    ("near", 0, 0, 0), ("own", 0, 1, 1), ("near", 0, 0, 1), ("own", 0, 0, 2), ("near", 0, 0, 2), ("near", 0, 0, 3),
    ("own", 0, 1, 2), ("own", 0, 0, 3), ("select", 0, 1, 1), ("near", 0, 1, 0), ("weigh", 0, 1), ("expert", 0, 0, 1),
    ("near", 0, 1, 1), ("weigh", 0, 0), ("turn", 0, 0, 2), ("near", 0, 1, 2), ("near", 0, 1, 3), ("expert", 0, 0, 0),
    ("turn", 0, 0, 3), ("finish", 0, 0, 0), ("own", 0, 1, 3), ("finish", 0, 0, 1), ("expert", 0, 1, 1), ("expert", 0, 1, 0),
    ("combine", 0, 0, 0), ("combine", 0, 0, 1), ("finish", 0, 1, 0), ("turn", 0, 1, 2), ("combine", 0, 0, 2),
    ("combine", 0, 0, 3), ("select", 1, 0, 1), ("turn", 0, 1, 3), ("take", 1, 0, 0), ("finish", 0, 1, 1), ("select", 1, 0, 0),
    ("combine", 0, 1, 0), ("own", 1, 0, 0), ("take", 1, 0, 1), ("own", 1, 0, 1), ("take", 1, 0, 2), ("combine", 0, 1, 1),
    ("own", 1, 0, 2), ("take", 1, 0, 3), ("combine", 0, 1, 2), ("own", 1, 0, 3), ("combine", 0, 1, 3), ("take", 1, 1, 0),
    ("near", 1, 0, 0), ("take", 1, 1, 1), ("select", 1, 1, 0), ("own", 1, 1, 0), ("near", 1, 0, 1), ("weigh", 1, 0),
    ("near", 1, 0, 2), ("near", 1, 0, 3), ("take", 1, 1, 2), ("expert", 1, 0, 0), ("take", 1, 1, 3), ("select", 1, 1, 1),
    ("own", 1, 1, 1), ("near", 1, 1, 0), ("near", 1, 1, 1), ("expert", 1, 0, 1), ("near", 1, 1, 2), ("turn", 1, 0, 2),
    ("near", 1, 1, 3), ("turn", 1, 0, 3), ("own", 1, 1, 2), ("finish", 1, 0, 0), ("own", 1, 1, 3), ("expert", 1, 1, 1),
    ("finish", 1, 0, 1), ("expert", 1, 1, 0), ("turn", 1, 1, 2), ("combine", 1, 0, 0), ("turn", 1, 1, 3), ("finish", 1, 1, 0),
    ("combine", 1, 0, 1), ("combine", 1, 0, 2), ("finish", 1, 1, 1), ("weigh", 1, 1), ("combine", 1, 0, 3),
    ("combine", 1, 1, 0), ("combine", 1, 1, 1), ("combine", 1, 1, 2), ("combine", 1, 1, 3),
)


def relay(
    pipe_count,
    a_in, b_in, later_in, routes, gain, router, gate_in, up_in, down_in,
    a_out, b_out,
    gate, up, down, own_x, near_x, near_routes, normed, packed, got, part, crossed, returned, near_returned, turned, met, outs, rows, hidden,
    pick, spread, near_spread, placed_at, weight,
    load_sem, weight_sem, store_sem, route_send, route_recv, x_send, x_recv, chunk_send, chunk_recv, cross_send, cross_recv,
    back_send, back_recv, near_back_send, near_back_recv, turn_send, turn_recv, pipe_send, pipe_recv,
):
    tokens, width = own_x.shape[2:]
    block = PARTS * HEAD
    tails = PARTS * TAIL
    tiles = width // TILE
    pieces = pieces_of(width)
    every = range(len(pieces))
    loaded = set()
    pipe, place = lax.axis_index("pipe"), lax.axis_index("expert")
    y, x = place // SIDE, place % SIDE
    near = y * SIDE + x + 1 - 2 * (x % 2)
    inputs, results = (a_in, b_in), (a_out, b_out)

    def plain(p):
        return slice(pieces[p][0] * TILE, pieces[p][1] * TILE)

    def wide(p):
        return slice(pieces[p][0] * LONG, pieces[p][1] * LONG)

    first_direct = pieces[DIRECT][0]

    def late(p):
        return slice((pieces[p][0] - first_direct) * TILE, (pieces[p][1] - first_direct) * TILE)

    def late_wide(p):
        return slice((pieces[p][0] - first_direct) * LONG, (pieces[p][1] - first_direct) * LONG)

    def partner(k, way):
        column = x + (k // SIDE) * (SIDE - 1 - 2 * x)
        return ((y + SIDE + way * (k % SIDE)) % SIDE) * SIDE + column

    def chunk(k):
        return pl.ds(pl.multiple_of(k * HEAD, HEAD), HEAD)

    def remote(source, target, send, recv, device):
        return pltpu.make_async_remote_copy(
            src_ref=source, dst_ref=target, send_sem=send, recv_sem=recv, device_id=device, device_id_type=MESH
        )

    def chunk_copy(g, h, p, k):
        return remote(
            packed.at[g, h, chunk(k), wide(p)], got.at[g, h, chunk(k), wide(p)],
            chunk_send.at[g, h, p, k], chunk_recv.at[g, h, p, k], (pipe, partner(k, 1)),
        )

    def back_copy(g, p, k):
        return remote(
            part.at[g, 0, chunk(k), wide(p)], returned.at[g, chunk(k), wide(p)],
            back_send.at[g, p, k], back_recv.at[g, p, k], (pipe, partner(k, -1)),
        )

    def near_back_copy(g, p, k):
        return remote(
            part.at[g, 1, chunk(k), wide(p)], near_returned.at[g, chunk(k), late_wide(p)],
            near_back_send.at[g, p - DIRECT, k], near_back_recv.at[g, p - DIRECT, k], (pipe, partner(k, -1)),
        )

    def turned_copy(g, p):
        return remote(
            turned.at[g, :, late(p)], met.at[g, :, late(p)], turn_send.at[g, p - DIRECT], turn_recv.at[g, p - DIRECT],
            (pipe, near),
        )

    def cross_copy(g, p):
        return remote(
            part.at[g, 1, :, wide(p)], crossed.at[g, :, wide(p)], cross_send.at[g, p], cross_recv.at[g, p], (pipe, near)
        )

    def x_copy(s, g, p):
        source = inputs[g].at[0, :, plain(p)] if s == 0 else own_x.at[s, g, :, plain(p)]
        return remote(source, near_x.at[s, g, :, plain(p)], x_send.at[g, p], x_recv.at[g, p], (pipe, near))

    def route_copy():
        return remote(routes, near_routes, route_send, route_recv, (pipe, near))

    def pipe_copy(g, p):
        return remote(
            outs.at[g, :, plain(p)], own_x.at[1, g, :, plain(p)], pipe_send.at[g, p], pipe_recv.at[g, p],
            (pipe + 1 - 2 * g, place),
        )

    def has_next(g):
        return pipe < pipe_count - 1 if g == 0 else pipe > 0

    def load_copy(g):
        return pltpu.make_async_copy(inputs[g].at[0], own_x.at[0, g], load_sem.at[g])

    def weight_copies(g):
        return [
            pltpu.make_async_copy(source.at[0, g], target.at[g], weight_sem.at[g, i])
            for i, (source, target) in enumerate(((gate_in, gate), (up_in, up), (down_in, down)))
        ]

    def store_copy(s, g, p):
        return pltpu.make_async_copy(outs.at[g, :, plain(p)], results[g].at[s, 0, :, plain(p)], store_sem.at[g, p])

    def later_copy(p):
        return pltpu.make_async_copy(later_in.at[0, :, plain(p)], own_x.at[1, 0, :, plain(p)], pipe_recv.at[0, p])

    def turn_copy(p):
        return pltpu.make_async_copy(outs.at[0, :, plain(p)], own_x.at[1, 1, :, plain(p)], pipe_recv.at[1, p])

    def each(first, last, action):
        lax.fori_loop(first, last, lambda k, carry: (action(k), carry)[1], 0)

    def slot_codes(chosen):
        hot = iota((PARTS, tokens), 0) == chosen
        upper = ones_where(iota((tokens, tokens), 0) <= iota((tokens, tokens), 1))
        seen = dot(ones_where(hot), upper)
        slot = jnp.sum(jnp.where(hot, seen - 1.0, 0.0), axis=0, keepdims=True)
        return chosen * 32 + slot.astype(I32)

    def selectors(codes, axis):
        shape = (block, tokens) if axis == 0 else (tokens, block)
        row = iota(shape, axis)
        k, low = row // HEAD, row % HEAD
        expert = 2 * ((y + k) % SIDE) + jnp.where(k >= SIDE, SIDE - 1 - x, x) // 2
        tail_hit = codes == expert * 32 + HEAD + low % TAIL
        return [ones_where(codes == expert * 32 + low)] + [ones_where(tail_hit & (low // TAIL == b)) for b in range(CELLS)]

    def select(s, g, h):
        chosen = (routes if h == 0 else near_routes)[2 * s + g:2 * s + g + 1, :]
        codes = slot_codes(chosen)
        for i, selector in enumerate(selectors(codes, 0)):
            pick[g, h, i] = selector
        codes_down = jnp.transpose(jnp.broadcast_to(codes.astype(F32), (tokens, tokens))).astype(I32)
        target = spread if h == 0 else near_spread
        for i, selector in enumerate(selectors(codes_down, 1)):
            target[g, i] = selector
        if h == 0:
            placed_at[g] = codes_down

    def normalize(source, target, gains, count):
        def one(i):
            at = pl.ds(pl.multiple_of(i * HEAD, HEAD), HEAD)
            values = source[at, :].astype(F32)
            mean_square = jnp.mean(values * values, axis=-1, keepdims=True)
            target[at, :] = (values * lax.rsqrt(mean_square + 1e-06) * gains).astype(BF16)

        each(0, count // HEAD, one)

    def weigh(s, g):
        normalize(own_x.at[s, g], normed, gain[...].astype(F32)[g:g + 1], tokens)
        logits = lax.dot_general(normed[...], router[g], (((1,), (1,)), ((), ())), preferred_element_type=F32)
        mine = iota((tokens, PARTS), 1) == placed_at[g, :, 0:PARTS] // 32
        logit = jnp.sum(jnp.where(mine, logits, 0.0), axis=-1, keepdims=True)
        weight[g] = jnp.broadcast_to(ROUTE_GAIN * jax.nn.sigmoid(logit), (tokens, LANES))

    def send_piece(s, g, h, p):
        source = (own_x if h == 0 else near_x).at[s, g]
        for c in range(*pieces[p]):
            values = source[:, c * TILE:(c + 1) * TILE]
            packed[g, h, :, c * LONG:c * LONG + TILE] = dot(pick[g, h, 0], values).astype(BF16)
            total = dot(pick[g, h, 1], values[:, :LANES])
            for b in range(1, CELLS):
                total = total + dot(pick[g, h, 1 + b], values[:, b * LANES:(b + 1) * LANES])
            packed[g, h, :, c * LONG + TILE:(c + 1) * LONG] = total.astype(BF16)
        each(1, PARTS, lambda k: chunk_copy(g, h, p, k).start())
        got[g, h, 0:HEAD, wide(p)] = packed[g, h, 0:HEAD, wide(p)]

    def send_own(s, g, p):
        send_piece(s, g, 0, p)

    def send_near(s, g, p):
        x_copy(s, g, p).wait()
        send_piece(s, g, 1, p)

    def wait_chunks(g, h):
        for p in every:
            each(1, PARTS, lambda k: chunk_copy(g, h, p, k).wait())

    def send_back(g, p):
        each(1, PARTS, lambda k: back_copy(g, p, k).start())
        returned[g, 0:HEAD, wide(p)] = part[g, 0, 0:HEAD, wide(p)]

    def expert(s, g, h):
        if g not in loaded:
            loaded.add(g)
            for copy in weight_copies(g):
                copy.wait()
        wait_chunks(g, h)
        out_row, in_row = iota((block, block), 0), iota((block, block), 1)
        gather = (out_row // TAIL % PARTS) * HEAD + (out_row // tails) * TAIL + out_row % TAIL
        scatter = ones_where(in_row == (out_row % HEAD // TAIL) * tails + (out_row // HEAD) * TAIL + out_row % TAIL)
        for c in range(tiles):
            rows[0:block, c * TILE:(c + 1) * TILE] = got[g, h, :, c * LONG:c * LONG + TILE]
        cells = jnp.concatenate([got[g, h, :, c * LONG + TILE:(c + 1) * LONG] for c in range(tiles)], axis=1)
        cells = dot(ones_where(in_row == gather), cells).astype(BF16)
        for c in range(tiles):
            for b in range(CELLS):
                at = c * TILE + b * LANES
                rows[block:, at:at + LANES] = cells[b * tails:(b + 1) * tails, c * LANES:(c + 1) * LANES]
        normalize(rows, rows, gain[...].astype(F32)[g:g + 1], block + tails)
        units = hidden.shape[1]
        inner = min(256, units)

        def widen(j):
            at = pl.ds(pl.multiple_of(j * inner, inner), inner)
            gate_val = dot(rows[...], gate[g, :, at])
            up_val = dot(rows[...], up[g, :, at])
            hidden[:, at] = (gate_val * jax.nn.sigmoid(gate_val) * up_val).astype(BF16)

        each(0, units // inner, widen)

        def narrow(c):
            value = dot(hidden[...], down[g, :, pl.ds(pl.multiple_of(c * TILE, TILE), TILE)]).astype(BF16)
            part[g, h, :, pl.ds(pl.multiple_of(c * LONG, LANES), TILE)] = value[:block]
            stacked = jnp.concatenate([value[block:, b * LANES:(b + 1) * LANES] for b in range(CELLS)], axis=0)
            part[g, h, :, pl.ds(pl.multiple_of(c * LONG + TILE, LANES), LANES)] = dot(scatter, stacked).astype(BF16)

        for p in every:
            each(*pieces[p], narrow)
            if p >= DIRECT and h == 1:
                each(1, PARTS, lambda k: near_back_copy(g, p, k).start())
                near_returned[g, 0:HEAD, late_wide(p)] = part[g, 1, 0:HEAD, wide(p)]
            elif p >= DIRECT:
                send_back(g, p)
            elif h == 1:
                cross_copy(g, p).start()

    def finish_cross(s, g, p):
        cross_copy(g, p).wait()
        for c in range(*pieces[p]):
            at = slice(c * LONG, (c + 1) * LONG)
            part[g, 0, :, at] = (part[g, 0, :, at].astype(F32) + crossed[g, :, at].astype(F32)).astype(BF16)
        send_back(g, p)

    def gathered(selector, source, at):
        cells = source[:, at + TILE:at + LONG]
        tail = jnp.concatenate([dot(selector[1 + b], cells) for b in range(CELLS)], axis=1)
        return dot(selector[0], source[:, at:at + TILE]) + tail

    def turn(s, g, p):
        each(1, PARTS, lambda k: near_back_copy(g, p, k).wait())
        for c in range(*pieces[p]):
            i = c - first_direct
            values = gathered(near_spread.at[g], near_returned.at[g], i * LONG)
            turned[g, :, i * TILE:(i + 1) * TILE] = values.astype(BF16)
        turned_copy(g, p).start()

    def combine(s, g, p):
        each(1, PARTS, lambda k: back_copy(g, p, k).wait())
        if p >= DIRECT:
            turned_copy(g, p).wait()
        if s == 1:
            store_copy(0, g, p).wait()
            pl.when(has_next(g))(lambda: pipe_copy(g, p).wait_send())
        for c in range(*pieces[p]):
            at = slice(c * TILE, (c + 1) * TILE)
            expert_out = gathered(spread.at[g], returned.at[g], c * LONG)
            if p >= DIRECT:
                expert_out = expert_out + met[g, :, (c - first_direct) * TILE:(c - first_direct + 1) * TILE].astype(F32)
            values = own_x[s, g, :, at].astype(F32)
            outs[g, :, at] = (values + weight[g, :, 0:1] * expert_out).astype(BF16)
        if s == 0:
            pl.when(has_next(g))(lambda: pipe_copy(g, p).start())
            if g == 0:
                pl.when(pipe == pipe_count - 1)(lambda: turn_copy(p).start())
        store_copy(s, g, p).start()

    def take(s, g, p):
        pltpu.make_async_copy(outs.at[g, :, plain(p)], own_x.at[s, g, :, plain(p)], pipe_recv.at[g, p]).wait()
        x_copy(s, g, p).start()

    for g in (0, 1):
        load_copy(g).start()
    for g in (0, 1):
        for copy in weight_copies(g):
            copy.start()

    @pl.when(pipe == 0)
    def _():
        for p in every:
            later_copy(p).start()

    barrier = pltpu.get_barrier_semaphore()

    def greet(device):
        pl.semaphore_signal(barrier, inc=1, device_id=device, device_id_type=MESH)

    each(1, PARTS, lambda k: greet((pipe, partner(k, 1))))
    greet((pipe, near))
    pl.when(pipe > 0)(lambda: greet((pipe - 1, place)))
    pl.when(pipe < pipe_count - 1)(lambda: greet((pipe + 1, place)))
    before, after = (pipe + pipe_count - 1) // pipe_count, (2 * pipe_count - 2 - pipe) // pipe_count
    pl.semaphore_wait(barrier, PARTS + before + after)

    route_copy().start()
    for g in (0, 1):
        for p in every:
            x_copy(0, g, p).start()
    route_copy().wait()
    for g in (0, 1):
        load_copy(g).wait()
    actions = dict(
        select=select, own=send_own, near=send_near, take=take, weigh=weigh, expert=expert, finish=finish_cross, turn=turn,
        combine=combine,
    )
    for name, *where in ORDER:
        actions[name](*where)
    for g in (0, 1):
        for p in every:
            store_copy(1, g, p).wait()


def solution(mesh):
    pipe_count = mesh.shape["pipe"]

    def body(a_init, b_init, incoming, routes, gain, router, w_gate, w_up, w_down):
        tokens, width = a_init.shape[1:]
        units = w_gate.shape[-1]
        long = width // TILE * LONG
        block = PARTS * HEAD
        pieces = pieces_of(width)
        count = len(pieces)
        late_tiles = width // TILE - pieces[DIRECT][0]
        steps = routes.shape[1]
        chosen = routes.reshape(steps * 2, tokens)
        whole = pl.BlockSpec(memory_space=pltpu.VMEM)
        outside = pl.BlockSpec(memory_space=pl.ANY)
        result = jax.ShapeDtypeStruct((steps, 1, tokens, width), BF16)
        dma = pltpu.SemaphoreType.DMA
        return pl.pallas_call(
            functools.partial(relay, pipe_count),
            out_shape=(result, result),
            in_specs=[outside] * 3 + [whole] * 3 + [outside] * 3,
            out_specs=(outside, outside),
            scratch_shapes=[
                pltpu.VMEM((2, width, units), BF16),
                pltpu.VMEM((2, width, units), BF16),
                pltpu.VMEM((2, units, width), BF16),
                pltpu.VMEM((2, 2, tokens, width), BF16),
                pltpu.VMEM((2, 2, tokens, width), BF16),
                pltpu.VMEM((steps * 2, tokens), I32),
                pltpu.VMEM((tokens, width), BF16),
                pltpu.VMEM((2, 2, block, long), BF16),
                pltpu.VMEM((2, 2, block, long), BF16),
                pltpu.VMEM((2, 2, block, long), BF16),
                pltpu.VMEM((2, block, long), BF16),
                pltpu.VMEM((2, block, long), BF16),
                pltpu.VMEM((2, block, late_tiles * LONG), BF16),
                pltpu.VMEM((2, tokens, late_tiles * TILE), BF16),
                pltpu.VMEM((2, tokens, late_tiles * TILE), BF16),
                pltpu.VMEM((2, tokens, width), BF16),
                pltpu.VMEM((block + PARTS * TAIL, width), BF16),
                pltpu.VMEM((block + PARTS * TAIL, units), BF16),
                pltpu.VMEM((2, 2, 1 + CELLS, block, tokens), BF16),
                pltpu.VMEM((2, 1 + CELLS, tokens, block), BF16),
                pltpu.VMEM((2, 1 + CELLS, tokens, block), BF16),
                pltpu.VMEM((2, tokens, tokens), I32),
                pltpu.VMEM((2, tokens, LANES), F32),
                dma((2,)),
                dma((2, 3)),
                dma((2, count)),
                dma,
                dma,
                dma((2, count)),
                dma((2, count)),
                dma((2, 2, count, PARTS)),
                dma((2, 2, count, PARTS)),
                dma((2, count)),
                dma((2, count)),
                dma((2, count, PARTS)),
                dma((2, count, PARTS)),
                dma((2, count - DIRECT, PARTS)),
                dma((2, count - DIRECT, PARTS)),
                dma((2, count - DIRECT)),
                dma((2, count - DIRECT)),
                dma((2, count)),
                dma((2, count)),
            ],
            compiler_params=pltpu.CompilerParams(
                collective_id=0, has_side_effects=True, vmem_limit_bytes=63 * 2**20
            ),
            cost_estimate=pl.CostEstimate(
                flops=4 * 320 * width * units * 6, bytes_accessed=6 * width * units * 2 * 2, transcendentals=0
            ),
        )(a_init, b_init, incoming, chosen, gain[0], jnp.swapaxes(router[0], 1, 2), w_gate, w_up, w_down)

    placed = (
        P("pipe", "expert", None),
        P("pipe", "expert", None),
        P(None, "expert", None),
        P("pipe", None, None, "expert", None),
        P("pipe", None, None),
        P("pipe", None, None, None),
        P("pipe", None, None, "expert"),
        P("pipe", None, None, "expert"),
        P("pipe", None, "expert", None),
    )
    return jax.shard_map(
        body,
        mesh=mesh,
        in_specs=placed,
        out_specs=(P(None, "pipe", "expert", None), P(None, "pipe", "expert", None)),
        check_vma=False,
    )
```

```python
import functools

import jax
import jax.numpy as jnp
from jax import lax
from jax.experimental import pallas as pl
from jax.experimental.pallas import tpu as pltpu
from jax.sharding import PartitionSpec as P

MESH = pl.DeviceIdType.MESH
F32, BF16, I32 = jnp.float32, jnp.bfloat16, jnp.int32
ROUTE_GAIN = 2.5
SIDE = 4
PARTS = 8
HEAD, TAIL = 16, 4
LANES, CELLS = 128, 4
TILE, LONG = CELLS * LANES, CELLS * LANES + LANES


def pieces_of(width):
    tiles = width // TILE
    cuts = [cut for cut in CUTS if cut < tiles] + [tiles]
    return list(zip(cuts[:-1], cuts[1:]))


CUTS = (0, 3, 5)
DIRECT = 2


def iota(shape, axis):
    return lax.broadcasted_iota(I32, shape, axis)


def ones_where(mask):
    return jnp.where(mask, 1.0, 0.0).astype(BF16)


def dot(left, right):
    return jnp.dot(left, right, preferred_element_type=F32)


ORDER = (
    ("select", 0, 1, 0), ("own", 0, 1, 0), ("select", 0, 0, 1), ("select", 0, 0, 0), ("own", 0, 0, 0), ("near", 0, 0, 0),
    ("weigh", 0, 0), ("own", 0, 0, 1), ("near", 0, 0, 1), ("near", 0, 0, 2), ("select", 0, 1, 1), ("own", 0, 0, 2),
    ("near", 0, 1, 0), ("expert", 0, 0, 1), ("near", 0, 1, 1), ("own", 0, 1, 1), ("near", 0, 1, 2), ("expert", 0, 0, 0),
    ("turn", 0, 0, 2), ("own", 0, 1, 2), ("finish", 0, 0, 0), ("weigh", 0, 1), ("expert", 0, 1, 1), ("finish", 0, 0, 1),
    ("expert", 0, 1, 0), ("combine", 0, 0, 0), ("finish", 0, 1, 0), ("combine", 0, 0, 1), ("turn", 0, 1, 2),
    ("combine", 0, 0, 2), ("finish", 0, 1, 1), ("take", 1, 0, 0), ("select", 1, 0, 0), ("combine", 0, 1, 0), ("own", 1, 0, 0),
    ("combine", 0, 1, 1), ("take", 1, 0, 1), ("own", 1, 0, 1), ("combine", 0, 1, 2), ("take", 1, 0, 2), ("select", 1, 0, 1),
    ("own", 1, 0, 2), ("near", 1, 0, 0), ("take", 1, 1, 0), ("select", 1, 1, 0), ("select", 1, 1, 1), ("take", 1, 1, 1),
    ("near", 1, 0, 1), ("near", 1, 0, 2), ("weigh", 1, 0), ("own", 1, 1, 0), ("take", 1, 1, 2), ("near", 1, 1, 0),
    ("expert", 1, 0, 1), ("near", 1, 1, 1), ("near", 1, 1, 2), ("own", 1, 1, 1), ("expert", 1, 0, 0), ("own", 1, 1, 2),
    ("weigh", 1, 1), ("expert", 1, 1, 1), ("finish", 1, 0, 0), ("turn", 1, 0, 2), ("expert", 1, 1, 0), ("finish", 1, 1, 0),
    ("finish", 1, 0, 1), ("combine", 1, 0, 0), ("finish", 1, 1, 1), ("turn", 1, 1, 2), ("combine", 1, 1, 0),
    ("combine", 1, 0, 1), ("combine", 1, 0, 2), ("combine", 1, 1, 1), ("combine", 1, 1, 2),
)


def relay(
    pipe_count,
    a_in, b_in, later_in, routes, gain, router, gate_in, up_in, down_in,
    a_out, b_out,
    gate, up, down, own_x, near_x, near_routes, normed, packed, got, part, crossed, returned, near_returned, turned, met, outs, rows, hidden,
    pick, spread, near_spread, placed_at, weight,
    load_sem, weight_sem, store_sem, route_send, route_recv, x_send, x_recv, chunk_send, chunk_recv, cross_send, cross_recv,
    back_send, back_recv, near_back_send, near_back_recv, turn_send, turn_recv, pipe_send, pipe_recv,
):
    tokens, width = own_x.shape[2:]
    block = PARTS * HEAD
    tails = PARTS * TAIL
    tiles = width // TILE
    pieces = pieces_of(width)
    every = range(len(pieces))
    loaded = set()
    pipe, place = lax.axis_index("pipe"), lax.axis_index("expert")
    y, x = place // SIDE, place % SIDE
    near = y * SIDE + x + 1 - 2 * (x % 2)
    inputs, results = (a_in, b_in), (a_out, b_out)

    def plain(p):
        return slice(pieces[p][0] * TILE, pieces[p][1] * TILE)

    def wide(p):
        return slice(pieces[p][0] * LONG, pieces[p][1] * LONG)

    first_direct = pieces[DIRECT][0]

    def late(p):
        return slice((pieces[p][0] - first_direct) * TILE, (pieces[p][1] - first_direct) * TILE)

    def late_wide(p):
        return slice((pieces[p][0] - first_direct) * LONG, (pieces[p][1] - first_direct) * LONG)

    def partner(k, way):
        column = x + (k // SIDE) * (SIDE - 1 - 2 * x)
        return ((y + SIDE + way * (k % SIDE)) % SIDE) * SIDE + column

    def chunk(k):
        return pl.ds(pl.multiple_of(k * HEAD, HEAD), HEAD)

    def remote(source, target, send, recv, device):
        return pltpu.make_async_remote_copy(
            src_ref=source, dst_ref=target, send_sem=send, recv_sem=recv, device_id=device, device_id_type=MESH
        )

    def chunk_copy(g, h, p, k):
        return remote(
            packed.at[g, h, chunk(k), wide(p)], got.at[g, h, chunk(k), wide(p)],
            chunk_send.at[g, h, p, k], chunk_recv.at[g, h, p, k], (pipe, partner(k, 1)),
        )

    def back_copy(g, p, k):
        return remote(
            part.at[g, 0, chunk(k), wide(p)], returned.at[g, chunk(k), wide(p)],
            back_send.at[g, p, k], back_recv.at[g, p, k], (pipe, partner(k, -1)),
        )

    def near_back_copy(g, p, k):
        return remote(
            part.at[g, 1, chunk(k), wide(p)], near_returned.at[g, chunk(k), late_wide(p)],
            near_back_send.at[g, p - DIRECT, k], near_back_recv.at[g, p - DIRECT, k], (pipe, partner(k, -1)),
        )

    def turned_copy(g, p):
        return remote(
            turned.at[g, :, late(p)], met.at[g, :, late(p)], turn_send.at[g, p - DIRECT], turn_recv.at[g, p - DIRECT],
            (pipe, near),
        )

    def cross_copy(g, p):
        return remote(
            part.at[g, 1, :, wide(p)], crossed.at[g, :, wide(p)], cross_send.at[g, p], cross_recv.at[g, p], (pipe, near)
        )

    def x_copy(s, g, p):
        source = inputs[g].at[0, :, plain(p)] if s == 0 else own_x.at[s, g, :, plain(p)]
        return remote(source, near_x.at[s, g, :, plain(p)], x_send.at[g, p], x_recv.at[g, p], (pipe, near))

    def route_copy():
        return remote(routes, near_routes, route_send, route_recv, (pipe, near))

    def pipe_copy(g, p):
        return remote(
            outs.at[g, :, plain(p)], own_x.at[1, g, :, plain(p)], pipe_send.at[g, p], pipe_recv.at[g, p],
            (pipe + 1 - 2 * g, place),
        )

    def has_next(g):
        return pipe < pipe_count - 1 if g == 0 else pipe > 0

    def load_copy(g):
        return pltpu.make_async_copy(inputs[g].at[0], own_x.at[0, g], load_sem.at[g])

    def weight_copies(g):
        return [
            pltpu.make_async_copy(source.at[0, g], target.at[g], weight_sem.at[g, i])
            for i, (source, target) in enumerate(((gate_in, gate), (up_in, up), (down_in, down)))
        ]

    def store_copy(s, g, p):
        return pltpu.make_async_copy(outs.at[g, :, plain(p)], results[g].at[s, 0, :, plain(p)], store_sem.at[g, p])

    def later_copy(p):
        return pltpu.make_async_copy(later_in.at[0, :, plain(p)], own_x.at[1, 0, :, plain(p)], pipe_recv.at[0, p])

    def turn_copy(p):
        return pltpu.make_async_copy(outs.at[0, :, plain(p)], own_x.at[1, 1, :, plain(p)], pipe_recv.at[1, p])

    def each(first, last, action):
        lax.fori_loop(first, last, lambda k, carry: (action(k), carry)[1], 0)

    def slot_codes(chosen):
        hot = iota((PARTS, tokens), 0) == chosen
        upper = ones_where(iota((tokens, tokens), 0) <= iota((tokens, tokens), 1))
        seen = dot(ones_where(hot), upper)
        slot = jnp.sum(jnp.where(hot, seen - 1.0, 0.0), axis=0, keepdims=True)
        return chosen * 32 + slot.astype(I32)

    def selectors(codes, axis):
        shape = (block, tokens) if axis == 0 else (tokens, block)
        row = iota(shape, axis)
        k, low = row // HEAD, row % HEAD
        expert = 2 * ((y + k) % SIDE) + jnp.where(k >= SIDE, SIDE - 1 - x, x) // 2
        tail_hit = codes == expert * 32 + HEAD + low % TAIL
        return [ones_where(codes == expert * 32 + low)] + [ones_where(tail_hit & (low // TAIL == b)) for b in range(CELLS)]

    def select(s, g, h):
        chosen = (routes if h == 0 else near_routes)[2 * s + g:2 * s + g + 1, :]
        codes = slot_codes(chosen)
        for i, selector in enumerate(selectors(codes, 0)):
            pick[g, h, i] = selector
        codes_down = jnp.transpose(jnp.broadcast_to(codes.astype(F32), (tokens, tokens))).astype(I32)
        target = spread if h == 0 else near_spread
        for i, selector in enumerate(selectors(codes_down, 1)):
            target[g, i] = selector
        if h == 0:
            placed_at[g] = codes_down

    def normalize(source, target, gains, count):
        def one(i):
            at = pl.ds(pl.multiple_of(i * HEAD, HEAD), HEAD)
            values = source[at, :].astype(F32)
            mean_square = jnp.mean(values * values, axis=-1, keepdims=True)
            target[at, :] = (values * lax.rsqrt(mean_square + 1e-06) * gains).astype(BF16)

        each(0, count // HEAD, one)

    def weigh(s, g):
        normalize(own_x.at[s, g], normed, gain[...].astype(F32)[g:g + 1], tokens)
        logits = lax.dot_general(normed[...], router[g], (((1,), (1,)), ((), ())), preferred_element_type=F32)
        mine = iota((tokens, PARTS), 1) == placed_at[g, :, 0:PARTS] // 32
        logit = jnp.sum(jnp.where(mine, logits, 0.0), axis=-1, keepdims=True)
        weight[g] = jnp.broadcast_to(ROUTE_GAIN * jax.nn.sigmoid(logit), (tokens, LANES))

    def send_piece(s, g, h, p):
        source = (own_x if h == 0 else near_x).at[s, g]
        for c in range(*pieces[p]):
            values = source[:, c * TILE:(c + 1) * TILE]
            packed[g, h, :, c * LONG:c * LONG + TILE] = dot(pick[g, h, 0], values).astype(BF16)
            total = dot(pick[g, h, 1], values[:, :LANES])
            for b in range(1, CELLS):
                total = total + dot(pick[g, h, 1 + b], values[:, b * LANES:(b + 1) * LANES])
            packed[g, h, :, c * LONG + TILE:(c + 1) * LONG] = total.astype(BF16)
        each(1, PARTS, lambda k: chunk_copy(g, h, p, k).start())
        got[g, h, 0:HEAD, wide(p)] = packed[g, h, 0:HEAD, wide(p)]

    def send_own(s, g, p):
        send_piece(s, g, 0, p)

    def send_near(s, g, p):
        x_copy(s, g, p).wait()
        send_piece(s, g, 1, p)

    def wait_chunks(g, h):
        for p in every:
            each(1, PARTS, lambda k: chunk_copy(g, h, p, k).wait())

    def send_back(g, p):
        each(1, PARTS, lambda k: back_copy(g, p, k).start())
        returned[g, 0:HEAD, wide(p)] = part[g, 0, 0:HEAD, wide(p)]

    def expert(s, g, h):
        if g not in loaded:
            loaded.add(g)
            for copy in weight_copies(g):
                copy.wait()
        wait_chunks(g, h)
        out_row, in_row = iota((block, block), 0), iota((block, block), 1)
        gather = (out_row // TAIL % PARTS) * HEAD + (out_row // tails) * TAIL + out_row % TAIL
        scatter = ones_where(in_row == (out_row % HEAD // TAIL) * tails + (out_row // HEAD) * TAIL + out_row % TAIL)
        for c in range(tiles):
            rows[0:block, c * TILE:(c + 1) * TILE] = got[g, h, :, c * LONG:c * LONG + TILE]
        cells = jnp.concatenate([got[g, h, :, c * LONG + TILE:(c + 1) * LONG] for c in range(tiles)], axis=1)
        cells = dot(ones_where(in_row == gather), cells).astype(BF16)
        for c in range(tiles):
            for b in range(CELLS):
                at = c * TILE + b * LANES
                rows[block:, at:at + LANES] = cells[b * tails:(b + 1) * tails, c * LANES:(c + 1) * LANES]
        normalize(rows, rows, gain[...].astype(F32)[g:g + 1], block + tails)
        units = hidden.shape[1]
        inner = min(256, units)

        def widen(j):
            at = pl.ds(pl.multiple_of(j * inner, inner), inner)
            gate_val = dot(rows[...], gate[g, :, at])
            up_val = dot(rows[...], up[g, :, at])
            hidden[:, at] = (gate_val * jax.nn.sigmoid(gate_val) * up_val).astype(BF16)

        each(0, units // inner, widen)

        def narrow(c):
            value = dot(hidden[...], down[g, :, pl.ds(pl.multiple_of(c * TILE, TILE), TILE)]).astype(BF16)
            part[g, h, :, pl.ds(pl.multiple_of(c * LONG, LANES), TILE)] = value[:block]
            stacked = jnp.concatenate([value[block:, b * LANES:(b + 1) * LANES] for b in range(CELLS)], axis=0)
            part[g, h, :, pl.ds(pl.multiple_of(c * LONG + TILE, LANES), LANES)] = dot(scatter, stacked).astype(BF16)

        for p in every:
            each(*pieces[p], narrow)
            if p >= DIRECT and h == 1:
                each(1, PARTS, lambda k: near_back_copy(g, p, k).start())
                near_returned[g, 0:HEAD, late_wide(p)] = part[g, 1, 0:HEAD, wide(p)]
            elif p >= DIRECT:
                send_back(g, p)
            elif h == 1:
                cross_copy(g, p).start()

    def finish_cross(s, g, p):
        cross_copy(g, p).wait()
        for c in range(*pieces[p]):
            at = slice(c * LONG, (c + 1) * LONG)
            part[g, 0, :, at] = (part[g, 0, :, at].astype(F32) + crossed[g, :, at].astype(F32)).astype(BF16)
        send_back(g, p)

    def gathered(selector, source, at):
        cells = source[:, at + TILE:at + LONG]
        tail = jnp.concatenate([dot(selector[1 + b], cells) for b in range(CELLS)], axis=1)
        return dot(selector[0], source[:, at:at + TILE]) + tail

    def turn(s, g, p):
        each(1, PARTS, lambda k: near_back_copy(g, p, k).wait())
        for c in range(*pieces[p]):
            i = c - first_direct
            values = gathered(near_spread.at[g], near_returned.at[g], i * LONG)
            turned[g, :, i * TILE:(i + 1) * TILE] = values.astype(BF16)
        turned_copy(g, p).start()

    def combine(s, g, p):
        each(1, PARTS, lambda k: back_copy(g, p, k).wait())
        if p >= DIRECT:
            turned_copy(g, p).wait()
        if s == 1:
            store_copy(0, g, p).wait()
            pl.when(has_next(g))(lambda: pipe_copy(g, p).wait_send())
        for c in range(*pieces[p]):
            at = slice(c * TILE, (c + 1) * TILE)
            expert_out = gathered(spread.at[g], returned.at[g], c * LONG)
            if p >= DIRECT:
                expert_out = expert_out + met[g, :, (c - first_direct) * TILE:(c - first_direct + 1) * TILE].astype(F32)
            values = own_x[s, g, :, at].astype(F32)
            outs[g, :, at] = (values + weight[g, :, 0:1] * expert_out).astype(BF16)
        if s == 0:
            pl.when(has_next(g))(lambda: pipe_copy(g, p).start())
            if g == 0:
                pl.when(pipe == pipe_count - 1)(lambda: turn_copy(p).start())
        store_copy(s, g, p).start()

    def take(s, g, p):
        pltpu.make_async_copy(outs.at[g, :, plain(p)], own_x.at[s, g, :, plain(p)], pipe_recv.at[g, p]).wait()
        x_copy(s, g, p).start()

    for g in (0, 1):
        load_copy(g).start()
    for g in (0, 1):
        for copy in weight_copies(g):
            copy.start()

    @pl.when(pipe == 0)
    def _():
        for p in every:
            later_copy(p).start()

    barrier = pltpu.get_barrier_semaphore()

    def greet(device):
        pl.semaphore_signal(barrier, inc=1, device_id=device, device_id_type=MESH)

    each(1, PARTS, lambda k: greet((pipe, partner(k, 1))))
    greet((pipe, near))
    pl.when(pipe > 0)(lambda: greet((pipe - 1, place)))
    pl.when(pipe < pipe_count - 1)(lambda: greet((pipe + 1, place)))
    before, after = (pipe + pipe_count - 1) // pipe_count, (2 * pipe_count - 2 - pipe) // pipe_count
    pl.semaphore_wait(barrier, PARTS + before + after)

    route_copy().start()
    for g in (0, 1):
        for p in every:
            x_copy(0, g, p).start()
    route_copy().wait()
    for g in (0, 1):
        load_copy(g).wait()
    actions = dict(
        select=select, own=send_own, near=send_near, take=take, weigh=weigh, expert=expert, finish=finish_cross, turn=turn,
        combine=combine,
    )
    for name, *where in ORDER:
        actions[name](*where)
    for g in (0, 1):
        for p in every:
            store_copy(1, g, p).wait()


def solution(mesh):
    pipe_count = mesh.shape["pipe"]

    def body(a_init, b_init, incoming, routes, gain, router, w_gate, w_up, w_down):
        tokens, width = a_init.shape[1:]
        units = w_gate.shape[-1]
        long = width // TILE * LONG
        block = PARTS * HEAD
        pieces = pieces_of(width)
        count = len(pieces)
        late_tiles = width // TILE - pieces[DIRECT][0]
        steps = routes.shape[1]
        chosen = routes.reshape(steps * 2, tokens)
        whole = pl.BlockSpec(memory_space=pltpu.VMEM)
        outside = pl.BlockSpec(memory_space=pl.ANY)
        result = jax.ShapeDtypeStruct((steps, 1, tokens, width), BF16)
        dma = pltpu.SemaphoreType.DMA
        return pl.pallas_call(
            functools.partial(relay, pipe_count),
            out_shape=(result, result),
            in_specs=[outside] * 3 + [whole] * 3 + [outside] * 3,
            out_specs=(outside, outside),
            scratch_shapes=[
                pltpu.VMEM((2, width, units), BF16),
                pltpu.VMEM((2, width, units), BF16),
                pltpu.VMEM((2, units, width), BF16),
                pltpu.VMEM((2, 2, tokens, width), BF16),
                pltpu.VMEM((2, 2, tokens, width), BF16),
                pltpu.VMEM((steps * 2, tokens), I32),
                pltpu.VMEM((tokens, width), BF16),
                pltpu.VMEM((2, 2, block, long), BF16),
                pltpu.VMEM((2, 2, block, long), BF16),
                pltpu.VMEM((2, 2, block, long), BF16),
                pltpu.VMEM((2, block, long), BF16),
                pltpu.VMEM((2, block, long), BF16),
                pltpu.VMEM((2, block, late_tiles * LONG), BF16),
                pltpu.VMEM((2, tokens, late_tiles * TILE), BF16),
                pltpu.VMEM((2, tokens, late_tiles * TILE), BF16),
                pltpu.VMEM((2, tokens, width), BF16),
                pltpu.VMEM((block + PARTS * TAIL, width), BF16),
                pltpu.VMEM((block + PARTS * TAIL, units), BF16),
                pltpu.VMEM((2, 2, 1 + CELLS, block, tokens), BF16),
                pltpu.VMEM((2, 1 + CELLS, tokens, block), BF16),
                pltpu.VMEM((2, 1 + CELLS, tokens, block), BF16),
                pltpu.VMEM((2, tokens, tokens), I32),
                pltpu.VMEM((2, tokens, LANES), F32),
                dma((2,)),
                dma((2, 3)),
                dma((2, count)),
                dma,
                dma,
                dma((2, count)),
                dma((2, count)),
                dma((2, 2, count, PARTS)),
                dma((2, 2, count, PARTS)),
                dma((2, count)),
                dma((2, count)),
                dma((2, count, PARTS)),
                dma((2, count, PARTS)),
                dma((2, count - DIRECT, PARTS)),
                dma((2, count - DIRECT, PARTS)),
                dma((2, count - DIRECT)),
                dma((2, count - DIRECT)),
                dma((2, count)),
                dma((2, count)),
            ],
            compiler_params=pltpu.CompilerParams(
                collective_id=0, has_side_effects=True, vmem_limit_bytes=63 * 2**20
            ),
            cost_estimate=pl.CostEstimate(
                flops=4 * 320 * width * units * 6, bytes_accessed=6 * width * units * 2 * 2, transcendentals=0
            ),
        )(a_init, b_init, incoming, chosen, gain[0], jnp.swapaxes(router[0], 1, 2), w_gate, w_up, w_down)

    placed = (
        P("pipe", "expert", None),
        P("pipe", "expert", None),
        P(None, "expert", None),
        P("pipe", None, None, "expert", None),
        P("pipe", None, None),
        P("pipe", None, None, None),
        P("pipe", None, None, "expert"),
        P("pipe", None, None, "expert"),
        P("pipe", None, "expert", None),
    )
    return jax.shard_map(
        body,
        mesh=mesh,
        in_specs=placed,
        out_specs=(P(None, "pipe", "expert", None), P(None, "pipe", "expert", None)),
        check_vma=False,
    )
```

```python
import functools

import jax
import jax.numpy as jnp
from jax import lax
from jax.experimental import pallas as pl
from jax.experimental.pallas import tpu as pltpu
from jax.sharding import PartitionSpec as P

MESH = pl.DeviceIdType.MESH
F32, BF16, I32 = jnp.float32, jnp.bfloat16, jnp.int32
ROUTE_GAIN = 2.5
SIDE = 4
PARTS = 8
HEAD, TAIL = 16, 4
LANES, CELLS = 128, 4
TILE, LONG = CELLS * LANES, CELLS * LANES + LANES


def pieces_of(width):
    tiles = width // TILE
    cuts = [cut for cut in CUTS if cut < tiles] + [tiles]
    return list(zip(cuts[:-1], cuts[1:]))


CUTS = (0, 3, 5)
DIRECT = 2


def iota(shape, axis):
    return lax.broadcasted_iota(I32, shape, axis)


def ones_where(mask):
    return jnp.where(mask, 1.0, 0.0).astype(BF16)


def dot(left, right):
    return jnp.dot(left, right, preferred_element_type=F32)


ORDER = (
    ("select", 0, 1, 0), ("own", 0, 1, 0), ("select", 0, 0, 1), ("select", 0, 0, 0), ("own", 0, 0, 0), ("near", 0, 0, 0),
    ("weigh", 0, 0), ("own", 0, 0, 1), ("near", 0, 0, 1), ("near", 0, 0, 2), ("select", 0, 1, 1), ("own", 0, 0, 2),
    ("near", 0, 1, 0), ("expert", 0, 0, 1), ("near", 0, 1, 1), ("own", 0, 1, 1), ("near", 0, 1, 2), ("expert", 0, 0, 0),
    ("turn", 0, 0, 2), ("own", 0, 1, 2), ("finish", 0, 0, 0), ("weigh", 0, 1), ("expert", 0, 1, 1), ("finish", 0, 0, 1),
    ("expert", 0, 1, 0), ("combine", 0, 0, 0), ("finish", 0, 1, 0), ("combine", 0, 0, 1), ("turn", 0, 1, 2),
    ("combine", 0, 0, 2), ("finish", 0, 1, 1), ("take", 1, 0, 0), ("select", 1, 0, 0), ("combine", 0, 1, 0), ("own", 1, 0, 0),
    ("combine", 0, 1, 1), ("take", 1, 0, 1), ("own", 1, 0, 1), ("combine", 0, 1, 2), ("take", 1, 0, 2), ("select", 1, 0, 1),
    ("own", 1, 0, 2), ("near", 1, 0, 0), ("take", 1, 1, 0), ("select", 1, 1, 0), ("select", 1, 1, 1), ("take", 1, 1, 1),
    ("near", 1, 0, 1), ("near", 1, 0, 2), ("weigh", 1, 0), ("own", 1, 1, 0), ("take", 1, 1, 2), ("near", 1, 1, 0),
    ("expert", 1, 0, 1), ("near", 1, 1, 1), ("near", 1, 1, 2), ("own", 1, 1, 1), ("expert", 1, 0, 0), ("own", 1, 1, 2),
    ("weigh", 1, 1), ("expert", 1, 1, 1), ("finish", 1, 0, 0), ("turn", 1, 0, 2), ("expert", 1, 1, 0), ("finish", 1, 1, 0),
    ("finish", 1, 0, 1), ("combine", 1, 0, 0), ("finish", 1, 1, 1), ("turn", 1, 1, 2), ("combine", 1, 1, 0),
    ("combine", 1, 0, 1), ("combine", 1, 0, 2), ("combine", 1, 1, 1), ("combine", 1, 1, 2),
)


def relay(
    pipe_count,
    a_in, b_in, later_in, routes, gain, router, gate_in, up_in, down_in,
    a_out, b_out,
    gate, up, down, own_x, near_x, near_routes, normed, packed, got, part, crossed, returned, near_returned, turned, met, outs, rows, hidden,
    pick, spread, near_spread, placed_at, weight,
    load_sem, weight_sem, store_sem, route_send, route_recv, x_send, x_recv, chunk_send, chunk_recv, cross_send, cross_recv,
    back_send, back_recv, near_back_send, near_back_recv, turn_send, turn_recv, pipe_send, pipe_recv,
):
    tokens, width = own_x.shape[2:]
    block = PARTS * HEAD
    tails = PARTS * TAIL
    tiles = width // TILE
    pieces = pieces_of(width)
    every = range(len(pieces))
    loaded = set()
    pipe, place = lax.axis_index("pipe"), lax.axis_index("expert")
    y, x = place // SIDE, place % SIDE
    near = y * SIDE + x + 1 - 2 * (x % 2)
    inputs, results = (a_in, b_in), (a_out, b_out)

    def plain(p):
        return slice(pieces[p][0] * TILE, pieces[p][1] * TILE)

    def wide(p):
        return slice(pieces[p][0] * LONG, pieces[p][1] * LONG)

    first_direct = pieces[DIRECT][0]

    def late(p):
        return slice((pieces[p][0] - first_direct) * TILE, (pieces[p][1] - first_direct) * TILE)

    def late_wide(p):
        return slice((pieces[p][0] - first_direct) * LONG, (pieces[p][1] - first_direct) * LONG)

    def partner(k, way):
        column = x + (k // SIDE) * (SIDE - 1 - 2 * x)
        return ((y + SIDE + way * (k % SIDE)) % SIDE) * SIDE + column

    def chunk(k):
        return pl.ds(pl.multiple_of(k * HEAD, HEAD), HEAD)

    def remote(source, target, send, recv, device):
        return pltpu.make_async_remote_copy(
            src_ref=source, dst_ref=target, send_sem=send, recv_sem=recv, device_id=device, device_id_type=MESH
        )

    def chunk_copy(g, h, p, k):
        return remote(
            packed.at[g, h, chunk(k), wide(p)], got.at[g, h, chunk(k), wide(p)],
            chunk_send.at[g, h, p, k], chunk_recv.at[g, h, p, k], (pipe, partner(k, 1)),
        )

    def back_copy(g, p, k):
        return remote(
            part.at[g, 0, chunk(k), wide(p)], returned.at[g, chunk(k), wide(p)],
            back_send.at[g, p, k], back_recv.at[g, p, k], (pipe, partner(k, -1)),
        )

    def near_back_copy(g, p, k):
        return remote(
            part.at[g, 1, chunk(k), wide(p)], near_returned.at[g, chunk(k), late_wide(p)],
            near_back_send.at[g, p - DIRECT, k], near_back_recv.at[g, p - DIRECT, k], (pipe, partner(k, -1)),
        )

    def turned_copy(g, p):
        return remote(
            turned.at[g, :, late(p)], met.at[g, :, late(p)], turn_send.at[g, p - DIRECT], turn_recv.at[g, p - DIRECT],
            (pipe, near),
        )

    def cross_copy(g, p):
        return remote(
            part.at[g, 1, :, wide(p)], crossed.at[g, :, wide(p)], cross_send.at[g, p], cross_recv.at[g, p], (pipe, near)
        )

    def x_copy(s, g, p):
        source = inputs[g].at[0, :, plain(p)] if s == 0 else own_x.at[s, g, :, plain(p)]
        return remote(source, near_x.at[s, g, :, plain(p)], x_send.at[g, p], x_recv.at[g, p], (pipe, near))

    def route_copy():
        return remote(routes, near_routes, route_send, route_recv, (pipe, near))

    def pipe_copy(g, p):
        return remote(
            outs.at[g, :, plain(p)], own_x.at[1, g, :, plain(p)], pipe_send.at[g, p], pipe_recv.at[g, p],
            (pipe + 1 - 2 * g, place),
        )

    def has_next(g):
        return pipe < pipe_count - 1 if g == 0 else pipe > 0

    def load_copy(g):
        return pltpu.make_async_copy(inputs[g].at[0], own_x.at[0, g], load_sem.at[g])

    def weight_copies(g):
        return [
            pltpu.make_async_copy(source.at[0, g], target.at[g], weight_sem.at[g, i])
            for i, (source, target) in enumerate(((gate_in, gate), (up_in, up), (down_in, down)))
        ]

    def store_copy(s, g, p):
        return pltpu.make_async_copy(outs.at[g, :, plain(p)], results[g].at[s, 0, :, plain(p)], store_sem.at[g, p])

    def later_copy(p):
        return pltpu.make_async_copy(later_in.at[0, :, plain(p)], own_x.at[1, 0, :, plain(p)], pipe_recv.at[0, p])

    def turn_copy(p):
        return pltpu.make_async_copy(outs.at[0, :, plain(p)], own_x.at[1, 1, :, plain(p)], pipe_recv.at[1, p])

    def each(first, last, action):
        lax.fori_loop(first, last, lambda k, carry: (action(k), carry)[1], 0)

    def slot_codes(chosen):
        hot = iota((PARTS, tokens), 0) == chosen
        upper = ones_where(iota((tokens, tokens), 0) <= iota((tokens, tokens), 1))
        seen = dot(ones_where(hot), upper)
        slot = jnp.sum(jnp.where(hot, seen - 1.0, 0.0), axis=0, keepdims=True)
        return chosen * 32 + slot.astype(I32)

    def selectors(codes, axis):
        shape = (block, tokens) if axis == 0 else (tokens, block)
        row = iota(shape, axis)
        k, low = row // HEAD, row % HEAD
        expert = 2 * ((y + k) % SIDE) + jnp.where(k >= SIDE, SIDE - 1 - x, x) // 2
        tail_hit = codes == expert * 32 + HEAD + low % TAIL
        return [ones_where(codes == expert * 32 + low)] + [ones_where(tail_hit & (low // TAIL == b)) for b in range(CELLS)]

    def select(s, g, h):
        chosen = (routes if h == 0 else near_routes)[2 * s + g:2 * s + g + 1, :]
        codes = slot_codes(chosen)
        for i, selector in enumerate(selectors(codes, 0)):
            pick[g, h, i] = selector
        codes_down = jnp.transpose(jnp.broadcast_to(codes.astype(F32), (tokens, tokens))).astype(I32)
        target = spread if h == 0 else near_spread
        for i, selector in enumerate(selectors(codes_down, 1)):
            target[g, i] = selector
        if h == 0:
            placed_at[g] = codes_down

    def normalize(source, target, gains, count):
        def one(i):
            at = pl.ds(pl.multiple_of(i * HEAD, HEAD), HEAD)
            values = source[at, :].astype(F32)
            mean_square = jnp.mean(values * values, axis=-1, keepdims=True)
            target[at, :] = (values * lax.rsqrt(mean_square + 1e-06) * gains).astype(BF16)

        each(0, count // HEAD, one)

    def weigh(s, g):
        normalize(own_x.at[s, g], normed, gain[...].astype(F32)[g:g + 1], tokens)
        logits = lax.dot_general(normed[...], router[g], (((1,), (1,)), ((), ())), preferred_element_type=F32)
        mine = iota((tokens, PARTS), 1) == placed_at[g, :, 0:PARTS] // 32
        logit = jnp.sum(jnp.where(mine, logits, 0.0), axis=-1, keepdims=True)
        weight[g] = jnp.broadcast_to(ROUTE_GAIN * jax.nn.sigmoid(logit), (tokens, LANES))

    def send_piece(s, g, h, p):
        source = (own_x if h == 0 else near_x).at[s, g]
        for c in range(*pieces[p]):
            values = source[:, c * TILE:(c + 1) * TILE]
            packed[g, h, :, c * LONG:c * LONG + TILE] = dot(pick[g, h, 0], values).astype(BF16)
            total = dot(pick[g, h, 1], values[:, :LANES])
            for b in range(1, CELLS):
                total = total + dot(pick[g, h, 1 + b], values[:, b * LANES:(b + 1) * LANES])
            packed[g, h, :, c * LONG + TILE:(c + 1) * LONG] = total.astype(BF16)
        each(1, PARTS, lambda k: chunk_copy(g, h, p, k).start())
        got[g, h, 0:HEAD, wide(p)] = packed[g, h, 0:HEAD, wide(p)]

    def send_own(s, g, p):
        send_piece(s, g, 0, p)

    def send_near(s, g, p):
        x_copy(s, g, p).wait()
        send_piece(s, g, 1, p)

    def wait_chunks(g, h):
        for p in every:
            each(1, PARTS, lambda k: chunk_copy(g, h, p, k).wait())

    def send_back(g, p):
        each(1, PARTS, lambda k: back_copy(g, p, k).start())
        returned[g, 0:HEAD, wide(p)] = part[g, 0, 0:HEAD, wide(p)]

    def expert(s, g, h):
        if g not in loaded:
            loaded.add(g)
            for copy in weight_copies(g):
                copy.wait()
        wait_chunks(g, h)
        out_row, in_row = iota((block, block), 0), iota((block, block), 1)
        gather = (out_row // TAIL % PARTS) * HEAD + (out_row // tails) * TAIL + out_row % TAIL
        scatter = ones_where(in_row == (out_row % HEAD // TAIL) * tails + (out_row // HEAD) * TAIL + out_row % TAIL)
        for c in range(tiles):
            rows[0:block, c * TILE:(c + 1) * TILE] = got[g, h, :, c * LONG:c * LONG + TILE]
        cells = jnp.concatenate([got[g, h, :, c * LONG + TILE:(c + 1) * LONG] for c in range(tiles)], axis=1)
        cells = dot(ones_where(in_row == gather), cells).astype(BF16)
        for c in range(tiles):
            for b in range(CELLS):
                at = c * TILE + b * LANES
                rows[block:, at:at + LANES] = cells[b * tails:(b + 1) * tails, c * LANES:(c + 1) * LANES]
        normalize(rows, rows, gain[...].astype(F32)[g:g + 1], block + tails)
        units = hidden.shape[1]
        inner = min(256, units)

        def widen(j):
            at = pl.ds(pl.multiple_of(j * inner, inner), inner)
            gate_val = dot(rows[...], gate[g, :, at])
            up_val = dot(rows[...], up[g, :, at])
            hidden[:, at] = (gate_val * jax.nn.sigmoid(gate_val) * up_val).astype(BF16)

        each(0, units // inner, widen)

        def narrow(c):
            value = dot(hidden[...], down[g, :, pl.ds(pl.multiple_of(c * TILE, TILE), TILE)]).astype(BF16)
            part[g, h, :, pl.ds(pl.multiple_of(c * LONG, LANES), TILE)] = value[:block]
            stacked = jnp.concatenate([value[block:, b * LANES:(b + 1) * LANES] for b in range(CELLS)], axis=0)
            part[g, h, :, pl.ds(pl.multiple_of(c * LONG + TILE, LANES), LANES)] = dot(scatter, stacked).astype(BF16)

        for p in every:
            each(*pieces[p], narrow)
            if p >= DIRECT and h == 1:
                each(1, PARTS, lambda k: near_back_copy(g, p, k).start())
                near_returned[g, 0:HEAD, late_wide(p)] = part[g, 1, 0:HEAD, wide(p)]
            elif p >= DIRECT:
                send_back(g, p)
            elif h == 1:
                cross_copy(g, p).start()

    def finish_cross(s, g, p):
        cross_copy(g, p).wait()
        for c in range(*pieces[p]):
            at = slice(c * LONG, (c + 1) * LONG)
            part[g, 0, :, at] = (part[g, 0, :, at].astype(F32) + crossed[g, :, at].astype(F32)).astype(BF16)
        send_back(g, p)

    def gathered(selector, source, at):
        cells = source[:, at + TILE:at + LONG]
        tail = jnp.concatenate([dot(selector[1 + b], cells) for b in range(CELLS)], axis=1)
        return dot(selector[0], source[:, at:at + TILE]) + tail

    def turn(s, g, p):
        each(1, PARTS, lambda k: near_back_copy(g, p, k).wait())
        for c in range(*pieces[p]):
            i = c - first_direct
            values = gathered(near_spread.at[g], near_returned.at[g], i * LONG)
            turned[g, :, i * TILE:(i + 1) * TILE] = values.astype(BF16)
        turned_copy(g, p).start()

    def combine(s, g, p):
        each(1, PARTS, lambda k: back_copy(g, p, k).wait())
        if p >= DIRECT:
            turned_copy(g, p).wait()
        if s == 1:
            store_copy(0, g, p).wait()
            pl.when(has_next(g))(lambda: pipe_copy(g, p).wait_send())
        for c in range(*pieces[p]):
            at = slice(c * TILE, (c + 1) * TILE)
            expert_out = gathered(spread.at[g], returned.at[g], c * LONG)
            if p >= DIRECT:
                expert_out = expert_out + met[g, :, (c - first_direct) * TILE:(c - first_direct + 1) * TILE].astype(F32)
            values = own_x[s, g, :, at].astype(F32)
            outs[g, :, at] = (values + weight[g, :, 0:1] * expert_out).astype(BF16)
        if s == 0:
            pl.when(has_next(g))(lambda: pipe_copy(g, p).start())
            if g == 0:
                pl.when(pipe == pipe_count - 1)(lambda: turn_copy(p).start())
        store_copy(s, g, p).start()

    def take(s, g, p):
        pltpu.make_async_copy(outs.at[g, :, plain(p)], own_x.at[s, g, :, plain(p)], pipe_recv.at[g, p]).wait()
        x_copy(s, g, p).start()

    for g in (0, 1):
        load_copy(g).start()
    for g in (0, 1):
        for copy in weight_copies(g):
            copy.start()

    @pl.when(pipe == 0)
    def _():
        for p in every:
            later_copy(p).start()

    barrier = pltpu.get_barrier_semaphore()

    def greet(device):
        pl.semaphore_signal(barrier, inc=1, device_id=device, device_id_type=MESH)

    each(1, PARTS, lambda k: greet((pipe, partner(k, 1))))
    greet((pipe, near))
    pl.when(pipe > 0)(lambda: greet((pipe - 1, place)))
    pl.when(pipe < pipe_count - 1)(lambda: greet((pipe + 1, place)))
    before, after = (pipe + pipe_count - 1) // pipe_count, (2 * pipe_count - 2 - pipe) // pipe_count
    pl.semaphore_wait(barrier, PARTS + before + after)

    route_copy().start()
    for g in (0, 1):
        for p in every:
            x_copy(0, g, p).start()
    route_copy().wait()
    for g in (0, 1):
        load_copy(g).wait()
    actions = dict(
        select=select, own=send_own, near=send_near, take=take, weigh=weigh, expert=expert, finish=finish_cross, turn=turn,
        combine=combine,
    )
    for name, *where in ORDER:
        actions[name](*where)
    for g in (0, 1):
        for p in every:
            store_copy(1, g, p).wait()


def solution(mesh):
    pipe_count = mesh.shape["pipe"]

    def body(a_init, b_init, incoming, routes, gain, router, w_gate, w_up, w_down):
        tokens, width = a_init.shape[1:]
        units = w_gate.shape[-1]
        long = width // TILE * LONG
        block = PARTS * HEAD
        pieces = pieces_of(width)
        count = len(pieces)
        late_tiles = width // TILE - pieces[DIRECT][0]
        steps = routes.shape[1]
        chosen = routes.reshape(steps * 2, tokens)
        whole = pl.BlockSpec(memory_space=pltpu.VMEM)
        outside = pl.BlockSpec(memory_space=pl.ANY)
        result = jax.ShapeDtypeStruct((steps, 1, tokens, width), BF16)
        dma = pltpu.SemaphoreType.DMA
        made = pl.pallas_call(
            functools.partial(relay, pipe_count),
            out_shape=(result, result),
            in_specs=[outside] * 3 + [whole] * 3 + [outside] * 3,
            out_specs=(outside, outside),
            scratch_shapes=[
                pltpu.VMEM((2, width, units), BF16),
                pltpu.VMEM((2, width, units), BF16),
                pltpu.VMEM((2, units, width), BF16),
                pltpu.VMEM((2, 2, tokens, width), BF16),
                pltpu.VMEM((2, 2, tokens, width), BF16),
                pltpu.VMEM((steps * 2, tokens), I32),
                pltpu.VMEM((tokens, width), BF16),
                pltpu.VMEM((2, 2, block, long), BF16),
                pltpu.VMEM((2, 2, block, long), BF16),
                pltpu.VMEM((2, 2, block, long), BF16),
                pltpu.VMEM((2, block, long), BF16),
                pltpu.VMEM((2, block, long), BF16),
                pltpu.VMEM((2, block, late_tiles * LONG), BF16),
                pltpu.VMEM((2, tokens, late_tiles * TILE), BF16),
                pltpu.VMEM((2, tokens, late_tiles * TILE), BF16),
                pltpu.VMEM((2, tokens, width), BF16),
                pltpu.VMEM((block + PARTS * TAIL, width), BF16),
                pltpu.VMEM((block + PARTS * TAIL, units), BF16),
                pltpu.VMEM((2, 2, 1 + CELLS, block, tokens), BF16),
                pltpu.VMEM((2, 1 + CELLS, tokens, block), BF16),
                pltpu.VMEM((2, 1 + CELLS, tokens, block), BF16),
                pltpu.VMEM((2, tokens, tokens), I32),
                pltpu.VMEM((2, tokens, LANES), F32),
                dma((2,)),
                dma((2, 3)),
                dma((2, count)),
                dma,
                dma,
                dma((2, count)),
                dma((2, count)),
                dma((2, 2, count, PARTS)),
                dma((2, 2, count, PARTS)),
                dma((2, count)),
                dma((2, count)),
                dma((2, count, PARTS)),
                dma((2, count, PARTS)),
                dma((2, count - DIRECT, PARTS)),
                dma((2, count - DIRECT, PARTS)),
                dma((2, count - DIRECT)),
                dma((2, count - DIRECT)),
                dma((2, count)),
                dma((2, count)),
            ],
            compiler_params=pltpu.CompilerParams(
                collective_id=0, has_side_effects=True, vmem_limit_bytes=63 * 2**20
            ),
            cost_estimate=pl.CostEstimate(
                flops=4 * 320 * width * units * 6, bytes_accessed=6 * width * units * 2 * 2, transcendentals=0
            ),
        )(a_init, b_init, incoming, chosen, gain[0], jnp.swapaxes(router[0], 1, 2), w_gate, w_up, w_down)

        def hand_over(a_from, b_from, a_to, b_to, held, sems):
            rows = tokens // 4
            parts = [(n, m, pl.ds(q * rows, rows), sems.at[n, m, q]) for n in range(steps) for m in (0, 1) for q in range(4)]
            into = [
                pltpu.make_async_copy((a_from, b_from)[m].at[n, 0, at], held.at[n, m, at], sem) for n, m, at, sem in parts
            ]
            out = [pltpu.make_async_copy(held.at[n, m, at], (a_to, b_to)[m].at[n, 0, at], sem) for n, m, at, sem in parts]
            for copy in into:
                copy.start()
            for first, second in zip(into, out):
                first.wait()
                second.start()
            for copy in out:
                copy.wait()

        return pl.pallas_call(
            hand_over,
            out_shape=(result, result),
            in_specs=[outside] * 2,
            out_specs=(outside, outside),
            scratch_shapes=[pltpu.VMEM((steps, 2, tokens, width), BF16), dma((steps, 2, 4))],
        )(*made)


    placed = (
        P("pipe", "expert", None),
        P("pipe", "expert", None),
        P(None, "expert", None),
        P("pipe", None, None, "expert", None),
        P("pipe", None, None),
        P("pipe", None, None, None),
        P("pipe", None, None, "expert"),
        P("pipe", None, None, "expert"),
        P("pipe", None, "expert", None),
    )
    return jax.shard_map(
        body,
        mesh=mesh,
        in_specs=placed,
        out_specs=(P(None, "pipe", "expert", None), P(None, "pipe", "expert", None)),
        check_vma=False,
    )
```
